256 devices in a mesh: phase: 8 (over x, core), seq: 32 (over z, y).
Axes of the slice: x: 4, y: 4, z: 8, core: 2. Of those that a mesh axis runs over, the one named last changes fastest.
Arguments:
- patches: bfloat16 [8192, 1024], P('seq'), may hold values from -6 to 6
- ln_gain: float32 [1024], replicated, may hold values from 0.1 to 1.9
- kv_proj: bfloat16 [1024, 2, 3072], P(None, None, 'phase'), may hold values from -0.1875 to 0.1875
- query: bfloat16 [5120, 3072], P('seq', 'phase'), may hold values from -128 to 128
- text_kv: bfloat16 [2, 5120, 3072], P(None, 'seq', 'phase'), may hold values from -128 to 128
- type_bias: bfloat16 [2, 3072], P(None, 'phase'), may hold values from -3 to 3
- d_out: bfloat16 [5120, 3072], P('seq', 'phase'), may hold values from -6 to 6
- patch_counts: int32 [32], replicated, may hold values from 1 to 64, as said below
- image_offsets: int32 [32], replicated, may hold values from 0 to 5119, as said below
- token_types: int32 [5120], P('seq'), may hold values from 0 to 1
- segment_ids: int32 [5120], replicated, may hold values from 0 to 15, never falling along the last dimension, each value on 1 to 2720 neighbouring positions
Outputs:
- attended: bfloat16 [5120, 3072], P('seq', 'phase')
- d_query: bfloat16 [5120, 3072], P('seq', 'phase')
- d_text_kv: bfloat16 [2, 5120, 3072], P(None, 'seq', 'phase')
- d_kv_proj: float32 [1024, 2, 3072], P('seq', None, 'phase')
- d_patches: bfloat16 [8192, 1024], P('seq')
The draws below stay inside these ranges and needn't reach their ends.
Inputs may be any that keep to these rules, and one draw needn't show every extreme that they name: `patch_counts`: some image has exactly 64 real rows. Image f takes the positions image_offsets[f] to image_offsets[f] + patch_counts[f] - 1; these runs are disjoint, and each lies within one block of 160 positions starting at a multiple of 160. `segment_ids`: ids never fall along the sequence; each episode is a run of at most 2720 positions.
All inputs are finite; a program needn't handle non-finite values.
Results may differ from the reference program's by a relative error of at most 0.03.
The reference program's roundings to bfloat16 on the way count: a program that leaves them out, or rounds other values in their place, can miss the bound.
Values may be sent and summed in bfloat16 or wider, within the bound.
No kernel may reach another device: no remote copies, remote signals or barrier semaphores. Data moves between devices by JAX's collectives and lax.ppermute only.
A program may use at most 128 MiB of HBM per device.

```python
import math
import jax
import jax.numpy as jnp
import numpy as np
from jax import lax

D_ENC = 1024
HD = 128
HEADS = 24
HC = 3072
TOK_DEV = 160
TOKENS = 5120
FR_DEV = 1
FRAMES = 32
PAD = 256
PATCH_MOST = 64
EP_MOST = 2720
EPISODES = 16


def key_normals(key):
    return jax.random.normal(key, (TOKENS, HEADS * HD), jnp.float32)


def patch_lengths(key):
    key = jax.random.fold_in(key, 11)
    lengths = jax.random.randint(key, (FRAMES,), 1, PATCH_MOST + 1)
    chosen_frame = jax.random.randint(jax.random.fold_in(key, 1), (), 0, FRAMES)
    return jnp.where(jnp.arange(FRAMES) == chosen_frame, PATCH_MOST, lengths).astype(jnp.int32)


def draw_patch_counts(key, part):
    return patch_lengths(key)


def draw_image_offsets(key, part):
    lengths = patch_lengths(key)
    key = jax.random.fold_in(key, 3)
    shard_total = FRAMES // FR_DEV
    order = jax.random.permutation(jax.random.fold_in(key, 1), shard_total).astype(jnp.int32)
    chosen = jax.random.randint(jax.random.fold_in(key, 2), (), 0, shard_total)
    wanted = (chosen + shard_total // 2) % shard_total
    holder = jnp.argmax(order == wanted)
    previous = order[chosen]
    order = order.at[holder].set(previous)
    order = order.at[chosen].set(wanted)
    frame_ids = jnp.arange(FRAMES, dtype=jnp.int32)
    dest_shard = order[frame_ids // FR_DEV]
    slot_width = TOK_DEV // FR_DEV
    room = slot_width - lengths
    raw_bits = jax.random.randint(jax.random.fold_in(key, 4), (FRAMES,), 0, 1 << 20)
    within = raw_bits % (room + 1)
    return (dest_shard * TOK_DEV + frame_ids % FR_DEV * slot_width + within).astype(jnp.int32)


def draw_text_kv(key, part):
    base_normal = key_normals(key)
    key = jax.random.fold_in(key, 5)
    key_rows = base_normal
    value_rows = jax.random.normal(key, (TOKENS, HEADS * HD), jnp.float32)
    return jnp.stack([key_rows, value_rows]).astype(jnp.bfloat16)


def draw_query(key, part):
    key = jax.random.fold_in(key, 7)
    fresh = 3.0 * jax.random.normal(key, (TOKENS, HEADS * HD), jnp.float32)
    return fresh.astype(jnp.bfloat16)


def set_ends(values, stream_key, low, largest):
    extent = values.shape
    index_at = [jax.random.randint(jax.random.fold_in(stream_key, axis), (), 0, extent[axis]) for axis in range(len(extent))]
    values = values.at[tuple(index_at)].set(low)
    longest = extent.index(max(extent))
    index_at[longest] = (index_at[longest] + 1) % extent[longest]
    return values.at[tuple(index_at)].set(largest)


def steps_of(stream_key, extent, split, least, high):
    factor_of = 1.0
    for dim, shards_of in split:
        draws = jax.random.uniform(jax.random.fold_in(jax.random.fold_in(stream_key, 6), dim), (shards_of,), jnp.float32, least / len(split), high / len(split))
        factor_of = factor_of * jnp.repeat(jnp.exp(draws), extent[dim] // shards_of).reshape((-1,) + (1,) * (len(extent) - 1 - dim))
    return factor_of


def profile(count, total, most, lean):
    portions = [(1 << 20) // math.isqrt(grade ** lean) + 1 for grade in range(2, count + 1)]
    rest, holding = total - most - (count - 1), [1] * (count - 1)
    while rest > 0:
        free = [i for i in range(count - 1) if holding[i] < most]
        mass, remaining = sum([portions[i] for i in free]), rest
        for i in free:
            addition = min(most - holding[i], max(1, remaining * portions[i] // mass), rest)
            holding[i] = holding[i] + addition
            rest = rest - addition
    return np.array([most] + holding)


def ragged_sizes(key, count, total, reach, skew):
    if count == 2:
        one = jax.random.randint(key, (), max(1, total - reach), min(reach, total - 1) + 1)
        return jnp.stack([one, total - one])
    sizes = jnp.asarray(profile(count, total, reach, skew), jnp.int32)
    couples = (count - 1) // 2
    giver, sink = sizes[1:1 + 2 * couples:2], sizes[2:2 + 2 * couples:2]
    slack = jnp.minimum(giver - 1, reach - sink)
    shifted = jax.random.randint(jax.random.fold_in(key, 1), (couples,), 0, 1 << 20) % (slack + 1)
    sizes = sizes.at[1:1 + 2 * couples:2].set(giver - shifted).at[2:2 + 2 * couples:2].set(sink + shifted)
    return sizes[jax.random.permutation(jax.random.fold_in(key, 2), count)]


def gaussian(key, extent, spread, most, split=(), kind=jnp.bfloat16):
    drawn = jax.random.normal(key, extent, jnp.float32) * spread
    if len(split) > 0:
        drawn = steps_of(key, extent, split, -0.22, 0.18) * drawn
    return jnp.clip(drawn, min=-most, max=most).astype(kind)


def setup_inputs(seed: int = 0) -> dict:
    arg_keys = jax.random.split(jax.random.key(seed), 12)
    patches = gaussian(arg_keys[0], (FRAMES * PAD, D_ENC), 1.0, 6.0, ((0, 32),))
    ln_gain = jnp.clip(1.0 + 0.18 * jax.random.normal(arg_keys[1], (D_ENC,), jnp.float32), 0.1, 1.9)
    kv_proj = gaussian(arg_keys[2], (D_ENC, 2, HC), D_ENC ** -0.5, 0.1875, ((2, 8),))
    query = draw_query(jax.random.fold_in(arg_keys[11], 71), 0)
    text_kv = draw_text_kv(jax.random.fold_in(arg_keys[11], 71), 0)
    type_bias = gaussian(arg_keys[5], (2, HC), 0.5, 3.0, ((1, 8),))
    d_out = gaussian(arg_keys[6], (TOKENS, HC), 1.0, 6.0, ((0, 32), (1, 8)))
    patch_counts = draw_patch_counts(jax.random.fold_in(arg_keys[11], 71), 0)
    image_offsets = draw_image_offsets(jax.random.fold_in(arg_keys[11], 71), 0)
    token_types = set_ends(jax.random.randint(arg_keys[9], (TOKENS,), 0, 2), jax.random.fold_in(arg_keys[9], 1), 0, 1).astype(jnp.int32)
    segment_ids = jnp.searchsorted(jnp.cumsum(ragged_sizes(arg_keys[10], EPISODES, TOKENS, EP_MOST, 2)), jnp.arange(TOKENS), side="right").astype(jnp.int32)
    return dict(patches=patches, ln_gain=ln_gain, kv_proj=kv_proj, query=query, text_kv=text_kv, type_bias=type_bias, d_out=d_out, patch_counts=patch_counts, image_offsets=image_offsets, token_types=token_types, segment_ids=segment_ids)


EPSILON = 1e-05
NEGATIVE = -1e+30

def normalize_rows(patches):
    row_values = patches.astype(jnp.float32)
    center = row_values - lax.optimization_barrier(jnp.mean(row_values, axis=-1, keepdims=True))
    inverse = lax.rsqrt(lax.optimization_barrier(jnp.mean(center * center, axis=-1, keepdims=True)) + EPSILON)
    return (center * inverse, inverse)

def reference(patches, ln_gain, kv_proj, query, text_kv, type_bias, d_out, patch_counts, image_offsets, token_types, segment_ids):
    head_cols = HEADS * HD
    score_scale_factor = 1.0 / math.sqrt(HD)
    scaled, inverse = normalize_rows(patches)
    norm_gain = ln_gain.astype(jnp.float32)
    normed = (scaled * norm_gain).astype(jnp.bfloat16)
    proj_matrix = kv_proj.reshape(D_ENC, 2 * head_cols)
    image_kv = jnp.dot(normed, proj_matrix, preferred_element_type=jnp.float32).astype(jnp.bfloat16)
    positions = jnp.arange(TOKENS, dtype=jnp.int32)
    starts = image_offsets.astype(jnp.int32)
    counts = patch_counts.astype(jnp.int32)
    inside = (positions[:, None] >= starts[None, :]) & (positions[:, None] < starts[None, :] + counts[None, :])
    is_image = jnp.any(inside, axis=1)
    frame_ids = jnp.arange(FRAMES, dtype=jnp.int32)
    frame_of = lax.optimization_barrier(jnp.sum(jnp.where(inside, frame_ids[None, :], 0), axis=1)).astype(jnp.int32)
    row_of = (positions - lax.optimization_barrier(jnp.sum(jnp.where(inside, starts[None, :], 0), axis=1))).astype(jnp.int32)
    source = jnp.where(is_image, frame_of * PAD + row_of, 0).astype(jnp.int32)
    routed = jnp.take(image_kv, source, axis=0)
    bias_rows = jnp.where(token_types[:, None] == 1, type_bias[1].astype(jnp.float32)[None, :], type_bias[0].astype(jnp.float32)[None, :])
    text_keys = (text_kv[0].astype(jnp.float32) + bias_rows).astype(jnp.bfloat16)
    keys = jnp.where(is_image[:, None], routed[:, :head_cols], text_keys)
    values = jnp.where(is_image[:, None], routed[:, head_cols:], text_kv[1])
    allowed = (segment_ids[:, None] == segment_ids[None, :]) & (positions[None, :] <= positions[:, None])
    blocks = TOKENS // TOK_DEV

    def head_pass(bundle):
        query_head, key_head, value_head, grad_head = bundle
        score = jnp.dot(query_head, key_head.T, preferred_element_type=jnp.float32) * score_scale_factor
        score = jnp.where(allowed, score, NEGATIVE)
        row_max = lax.optimization_barrier(jnp.max(score, axis=1, keepdims=True))
        weights = jnp.exp(score - row_max)
        prob_full = weights / lax.optimization_barrier(jnp.sum(weights, axis=1, keepdims=True))
        prob_low = prob_full.astype(jnp.bfloat16)
        output = jnp.dot(prob_low, value_head, preferred_element_type=jnp.float32).astype(jnp.bfloat16)
        d_prob = jnp.dot(grad_head, value_head.T, preferred_element_type=jnp.float32)
        delta = lax.optimization_barrier(jnp.sum(grad_head.astype(jnp.float32) * output.astype(jnp.float32), axis=1, keepdims=True))
        d_score = (prob_full * (d_prob - delta)).astype(jnp.bfloat16)
        d_query_head = (jnp.dot(d_score, key_head, preferred_element_type=jnp.float32) * score_scale_factor).astype(jnp.bfloat16)
        score_block_list = d_score.reshape(blocks, TOK_DEV, TOKENS).astype(jnp.float32)
        probability_block_list = prob_low.reshape(blocks, TOK_DEV, TOKENS).astype(jnp.float32)
        query_block_list = query_head.reshape(blocks, TOK_DEV, HD).astype(jnp.float32)
        gradient_block_list = grad_head.reshape(blocks, TOK_DEV, HD).astype(jnp.float32)
        key_term_list = (jnp.einsum('nsx,nse->nxe', score_block_list, query_block_list) * score_scale_factor).astype(jnp.bfloat16)
        value_term_list = jnp.einsum('nsx,nse->nxe', probability_block_list, gradient_block_list).astype(jnp.bfloat16)
        d_key_head = lax.optimization_barrier(jnp.sum(key_term_list.astype(jnp.float32), axis=0)).astype(jnp.bfloat16)
        d_value_head = lax.optimization_barrier(jnp.sum(value_term_list.astype(jnp.float32), axis=0)).astype(jnp.bfloat16)
        return (output, d_query_head, d_key_head, d_value_head)

    def split_heads(matrix):
        return matrix.reshape(TOKENS, HEADS, HD).transpose(1, 0, 2)

    def join_heads(stacked):
        return stacked.transpose(1, 0, 2).reshape(TOKENS, head_cols)
    results = lax.map(head_pass, (split_heads(query), split_heads(keys), split_heads(values), split_heads(d_out)))
    attended = join_heads(results[0])
    d_query = join_heads(results[1])
    d_keys = join_heads(results[2])
    d_values = join_heads(results[3])
    zero_rows = jnp.zeros_like(d_keys)
    d_text_kv = jnp.stack([jnp.where(is_image[:, None], zero_rows, d_keys), jnp.where(is_image[:, None], zero_rows, d_values)])
    grad_rows = jnp.concatenate([d_keys, d_values], axis=1).astype(jnp.float32)
    grad_rows = jnp.where(is_image[:, None], grad_rows, jnp.zeros_like(grad_rows))
    target = jnp.where(is_image, frame_of * PAD + row_of, FRAMES * PAD).astype(jnp.int32)
    d_image = jax.ops.segment_sum(grad_rows, target, FRAMES * PAD + 1)[:FRAMES * PAD].astype(jnp.bfloat16)
    d_kv_proj = lax.dot_general(normed, d_image, (((0,), (0,)), ((), ())), preferred_element_type=jnp.float32).reshape(D_ENC, 2, head_cols)
    d_normed = lax.dot_general(d_image, proj_matrix, (((1,), (1,)), ((), ())), preferred_element_type=jnp.float32)
    scaled_grad = d_normed * norm_gain
    d_patches = ((scaled_grad - lax.optimization_barrier(jnp.mean(scaled_grad, axis=-1, keepdims=True)) - scaled * lax.optimization_barrier(jnp.mean(scaled_grad * scaled, axis=-1, keepdims=True))) * inverse).astype(jnp.bfloat16)
    return (attended, d_query, d_text_kv, d_kv_proj, d_patches)
```

```python
import math

import jax
import jax.numpy as jnp
from jax import lax
from jax.experimental import pallas as pl
from jax.experimental.pallas import tpu as pltpu
from jax.sharding import Mesh
from jax.sharding import PartitionSpec as P

HD = 128
PAD = 256
PATCH_MOST = 64
EPISODES = 16
EPISODE_MOST = 2720
EPSILON = 1e-05
NEGATIVE = -1e30
CHUNK = 256

F32 = jnp.float32
BF16 = jnp.bfloat16


def dot_nt(a, b):
    return lax.dot_general(a, b, (((1,), (1,)), ((), ())), preferred_element_type=F32)


def dot_tn(a, b):
    return lax.dot_general(a, b, (((0,), (0,)), ((), ())), preferred_element_type=F32)


def dot_nn(a, b):
    return jnp.dot(a, b, preferred_element_type=F32)


def normalize_rows(patches):
    row_values = patches.astype(F32)
    center = row_values - jnp.mean(row_values, axis=-1, keepdims=True)
    inverse = lax.rsqrt(jnp.mean(center * center, axis=-1, keepdims=True) + EPSILON)
    return (center * inverse, inverse)


def vmem(limit=48):
    return pltpu.CompilerParams(vmem_limit_bytes=limit * 1024 * 1024)


def pack_kernel(heads, tok, patch_ref, gain_ref, proj_ref, q_ref, kv_ref, bias_ref, do_ref, type_ref,
                out_ref, normed_ref):
    scaled, _ = normalize_rows(patch_ref[...])
    normed = (scaled * gain_ref[...]).astype(BF16)
    normed_ref[...] = normed
    image = dot_nn(normed, proj_ref[...]).astype(BF16)
    cols = heads * HD
    bias = jnp.where(type_ref[...] == 1, bias_ref[1:2].astype(F32), bias_ref[0:1].astype(F32))
    keys = (kv_ref[0].astype(F32) + bias).astype(BF16)
    for h in range(heads):
        span = slice(h * HD, (h + 1) * HD)
        out_ref[h, 0:tok] = keys[:, span]
        out_ref[h, tok : 2 * tok] = kv_ref[1, :, span]
        out_ref[h, 2 * tok : 3 * tok] = q_ref[:, span]
        out_ref[h, 3 * tok : 4 * tok] = do_ref[:, span]
        out_ref[h, 4 * tok : 4 * tok + PATCH_MOST] = image[:, span]
        out_ref[h, 4 * tok + PATCH_MOST :] = image[:, cols + h * HD : cols + (h + 1) * HD]
    for h in range(heads, out_ref.shape[0]):
        out_ref[h] = jnp.zeros_like(out_ref[h])


def place_kernel(frames, meta_ref, rows_ref, out_ref, scratch):
    group = out_ref.shape[0]
    first = meta_ref[2 * frames] * group
    scratch[...] = jnp.zeros_like(scratch)
    row = lax.broadcasted_iota(jnp.int32, (PATCH_MOST, HD), 0)

    def one(f, carry):
        offset = meta_ref[f] - first

        @pl.when((offset >= 0) & (offset < group))
        def _():
            where = pl.ds(offset, PATCH_MOST)
            scratch[where] = jnp.where(
                row < meta_ref[frames + f], rows_ref[f].astype(F32), scratch[where]
            )

        return carry

    lax.fori_loop(0, frames, one, 0)
    out_ref[...] = scratch[0:group].astype(BF16)


def query_kernel(frames, tok, meta_ref, start_ref, g_ref, att_ref, dq_ref, own_ref, stat_ref,
                 kf, vf, kb, vb, qb, dob, s_ref, m_ref, l_ref, acc):
    group = att_ref.shape[0]
    total = kb.shape[0]
    scale = 1.0 / math.sqrt(HD)
    power = scale * math.log2(math.e)
    z = meta_ref[2 * frames]
    first_chunk = meta_ref[2 * frames + 2]
    last_chunk = meta_ref[2 * frames + 3]
    image_row = 4 * tok

    def text(b, carry):
        where = pl.ds(pl.multiple_of(b * tok, 32), tok)
        kf[where] = g_ref[b, 0:tok].astype(F32)
        vf[where] = g_ref[b, tok : 2 * tok].astype(F32)
        return carry

    lax.fori_loop(0, total // tok, text, 0)
    row = lax.broadcasted_iota(jnp.int32, (PATCH_MOST, HD), 0)

    def image(f, carry):
        where = pl.ds(meta_ref[f], PATCH_MOST)
        live = row < meta_ref[frames + f]
        kf[where] = jnp.where(live, g_ref[f, image_row : image_row + PATCH_MOST].astype(F32), kf[where])
        vf[where] = jnp.where(live, g_ref[f, image_row + PATCH_MOST :].astype(F32), vf[where])
        return carry

    lax.fori_loop(0, frames, image, 0)

    def low(c, carry):
        where = pl.ds(pl.multiple_of(c * CHUNK, CHUNK), CHUNK)
        kb[where] = kf[where].astype(BF16)
        vb[where] = vf[where].astype(BF16)
        return carry

    lax.fori_loop(0, total // CHUNK, low, 0)
    per = group // tok
    for i in range(per):
        qb[i * tok : (i + 1) * tok] = g_ref[z * per + i, 2 * tok : 3 * tok]
        dob[i * tok : (i + 1) * tok] = g_ref[z * per + i, 3 * tok : 4 * tok]
    own = pl.ds(pl.multiple_of(z * group, HD), group)
    own_ref[0] = kb[own]
    own_ref[1] = vb[own]

    m_ref[...] = jnp.full_like(m_ref, NEGATIVE)
    l_ref[...] = jnp.zeros_like(l_ref)
    acc[...] = jnp.zeros_like(acc)
    lane = lax.broadcasted_iota(jnp.int32, (group, CHUNK), 1)
    query_pos = z * group + lax.broadcasted_iota(jnp.int32, (group, 1), 0)
    start = start_ref[...]

    def chunk(c):
        return pl.ds(pl.multiple_of(c * CHUNK, CHUNK), CHUNK)

    def scores(c, carry):
        s = dot_nt(qb[...], kb[chunk(c)])
        pos = lane + c * CHUNK
        s = jnp.where((pos >= start) & (pos <= query_pos), s, NEGATIVE)
        s_ref[c - first_chunk] = s
        m_ref[...] = jnp.maximum(m_ref[...], jnp.maximum(s[:, :HD], s[:, HD:]))
        return carry

    lax.fori_loop(first_chunk, last_chunk, scores, 0)
    row_max = jnp.max(m_ref[...], axis=1, keepdims=True)
    m_ref[...] = jnp.broadcast_to(row_max, m_ref.shape)

    def weigh(c, carry):
        top = m_ref[...]
        w = jnp.exp2((s_ref[c - first_chunk] - jnp.concatenate([top, top], axis=1)) * power)
        s_ref[c - first_chunk] = w
        l_ref[...] += w[:, :HD] + w[:, HD:]
        acc[...] += dot_nn(w.astype(BF16), vb[chunk(c)])
        return carry

    lax.fori_loop(first_chunk, last_chunk, weigh, 0)
    inverse_sum = 1.0 / jnp.sum(l_ref[...], axis=1, keepdims=True)
    attended = (acc[...] * inverse_sum).astype(BF16)
    att_ref[...] = attended
    delta = jnp.sum(dob[...].astype(F32) * attended.astype(F32), axis=1, keepdims=True)
    acc[...] = jnp.zeros_like(acc)
    m_ref[...] = jnp.broadcast_to(inverse_sum, m_ref.shape)
    l_ref[...] = jnp.broadcast_to(delta, l_ref.shape)

    def back(c, carry):
        d_prob = dot_nt(dob[...], vb[chunk(c)])
        inv, dlt = m_ref[...], l_ref[...]
        p = s_ref[c - first_chunk] * jnp.concatenate([inv, inv], axis=1)
        d_score = (p * (d_prob - jnp.concatenate([dlt, dlt], axis=1))).astype(BF16)
        acc[...] += dot_nn(d_score, kb[chunk(c)])
        return carry

    lax.fori_loop(first_chunk, last_chunk, back, 0)
    dq_ref[...] = (acc[...] * scale).astype(BF16)
    which = lax.broadcasted_iota(jnp.int32, (group, HD), 1)
    table = jnp.where(which == 0, row_max, jnp.where(which == 1, inverse_sum, delta))
    for i in range(group // HD):
        stat_ref[i] = jnp.transpose(table[i * HD : (i + 1) * HD])[0:8]


def key_kernel(frames, tok, meta_ref, end_ref, g_ref, stat_ref, own_ref, norm_ref, dkv_ref, part_ref,
               qb, dob, dk, dv):
    group = own_ref.shape[1]
    total = qb.shape[0]
    scale = 1.0 / math.sqrt(HD)
    power = scale * math.log2(math.e)
    z = meta_ref[2 * frames]

    def text(b, carry):
        where = pl.ds(pl.multiple_of(b * tok, 32), tok)
        qb[where] = g_ref[b, 2 * tok : 3 * tok]
        dob[where] = g_ref[b, 3 * tok : 4 * tok]
        return carry

    lax.fori_loop(0, total // tok, text, 0)
    dk[...] = jnp.zeros_like(dk)
    dv[...] = jnp.zeros_like(dv)
    lane = lax.broadcasted_iota(jnp.int32, (group, CHUNK), 1)
    key_pos = z * group + lax.broadcasted_iota(jnp.int32, (group, 1), 0)
    end = end_ref[...]

    def step(c, carry):
        where = pl.ds(pl.multiple_of(c * CHUNK, CHUNK), CHUNK)
        stat = jnp.concatenate([stat_ref[2 * c], stat_ref[2 * c + 1]], axis=1)
        q, do = qb[where], dob[where]
        s = dot_nt(own_ref[0], q)
        pos = lane + c * CHUNK
        p = jnp.exp2((s - stat[0:1]) * power) * stat[1:2]
        p = jnp.where((pos >= key_pos) & (pos < end), p, 0.0)
        dv[...] += dot_nn(p.astype(BF16), do)
        d_prob = dot_nt(own_ref[1], do)
        d_score = (p * (d_prob - stat[2:3])).astype(BF16)
        dk[...] += dot_nn(d_score, q)
        return carry

    lax.fori_loop(meta_ref[2 * frames + 4], meta_ref[2 * frames + 5], step, 0)
    key_grad = (dk[...] * scale).astype(BF16)
    value_grad = dv[...].astype(BF16)
    dkv_ref[0] = key_grad
    dkv_ref[1] = value_grad
    both = jnp.concatenate([key_grad, value_grad], axis=1)
    for i in range(norm_ref.shape[0]):
        part_ref[i] = dot_tn(norm_ref[i], both).astype(BF16)


def unpack_kernel(heads, tok, r_ref, image_ref, proj_ref, att_ref, dq_ref, dtext_ref, dproj_ref, dn_ref):
    cols = heads * HD
    is_image = image_ref[...] == 1
    parts = [None] * (2 * heads)
    rows = dproj_ref.shape[0]
    for h in range(heads):
        span = slice(h * HD, (h + 1) * HD)
        att_ref[:, span] = r_ref[h, 0:tok]
        dq_ref[:, span] = r_ref[h, tok : 2 * tok]
        for c in range(2):
            grad = r_ref[h, (2 + c) * tok : (3 + c) * tok]
            zero = jnp.zeros_like(grad)
            dtext_ref[c, :, span] = jnp.where(is_image, zero, grad)
            parts[c * heads + h] = jnp.where(is_image, grad, zero)
            at = 4 * tok + c * rows
            dproj_ref[:, c * cols + h * HD : c * cols + (h + 1) * HD] = r_ref[h, at : at + rows].astype(F32)
    grads = jnp.concatenate(parts, axis=1)
    for i in range(dn_ref.shape[0]):
        dn_ref[i] = dot_nt(grads, proj_ref[i * HD : (i + 1) * HD]).astype(BF16)


def route_kernel(frames, tok, meta_ref, dn_ref, out_ref, scratch):
    first = meta_ref[2 * frames + 1] * tok
    total = dn_ref[0].astype(F32)
    for i in range(1, dn_ref.shape[0]):
        total = total + dn_ref[i].astype(F32)
    scratch[...] = jnp.zeros_like(scratch)
    scratch[0:tok] = total
    row = lax.broadcasted_iota(jnp.int32, (PATCH_MOST, HD), 0)

    def one(f, carry):
        offset = meta_ref[f] - first
        here = (offset >= 0) & (offset < tok)
        live = jnp.where(here, meta_ref[frames + f], 0)
        rows = scratch[pl.ds(jnp.where(here, offset, 0), PATCH_MOST)]
        out_ref[f] = jnp.where(row < live, rows, 0.0).astype(BF16)
        return carry

    lax.fori_loop(0, frames, one, 0)


def norm_grad_kernel(patch_ref, gain_ref, dn_ref, out_ref):
    scaled, inverse = normalize_rows(patch_ref[...])
    d_normed = jnp.concatenate([dn_ref[i] for i in range(dn_ref.shape[0])], axis=1).astype(F32)
    scaled_grad = d_normed * gain_ref[...]
    d_rows = (
        scaled_grad
        - jnp.mean(scaled_grad, axis=-1, keepdims=True)
        - scaled * jnp.mean(scaled_grad * scaled, axis=-1, keepdims=True)
    ) * inverse
    out_ref[0:PATCH_MOST] = d_rows.astype(BF16)
    out_ref[PATCH_MOST:] = jnp.zeros((out_ref.shape[0] - PATCH_MOST, out_ref.shape[1]), BF16)


def shards(patches, ln_gain, kv_proj, query, text_kv, type_bias, d_out, patch_counts, image_offsets,
           token_types, segment_ids):
    tok, cols = query.shape
    heads = cols // HD
    width = patches.shape[1]
    groups, per, sections = lax.axis_size("z"), lax.axis_size("y"), lax.axis_size("phase")
    frames = patch_counts.shape[0]
    blocks = groups * per
    group = per * tok
    total = blocks * tok
    z, y, section = lax.axis_index("z"), lax.axis_index("y"), lax.axis_index("phase")
    block = z * per + y
    smem = pl.BlockSpec(memory_space=pltpu.SMEM)
    whole = pl.BlockSpec(memory_space=pltpu.VMEM)

    def shape(dims, kind=BF16):
        return jax.ShapeDtypeStruct(dims, kind)

    ids = jnp.arange(EPISODES, dtype=jnp.int32)
    seg_first = jnp.sum((segment_ids[None, :] < ids[:, None]).astype(jnp.int32), axis=1)
    seg_end = jnp.sum((segment_ids[None, :] <= ids[:, None]).astype(jnp.int32), axis=1)
    own_seg = lax.dynamic_slice_in_dim(segment_ids, z * group, group)
    same = own_seg[:, None] == ids[None, :]
    start = jnp.sum(jnp.where(same, seg_first[None, :], 0), axis=1, keepdims=True)
    end = jnp.sum(jnp.where(same, seg_end[None, :], 0), axis=1, keepdims=True)
    scalars = jnp.stack([
        z,
        block,
        start[0, 0] // CHUNK,
        ((z + 1) * group + CHUNK - 1) // CHUNK,
        (z * group) // CHUNK,
        (end[group - 1, 0] + CHUNK - 1) // CHUNK,
    ]).astype(jnp.int32)
    meta = jnp.concatenate([image_offsets, patch_counts, scalars])
    positions = block * tok + jnp.arange(tok, dtype=jnp.int32)
    is_image = jnp.any(
        (positions[:, None] >= image_offsets[None, :])
        & (positions[:, None] < image_offsets[None, :] + patch_counts[None, :]),
        axis=1, keepdims=True,
    ).astype(jnp.int32)

    gain = ln_gain.reshape(1, width)
    proj = kv_proj.reshape(width, 2 * cols)
    used = patches[:PATCH_MOST]
    rows_each = 4 * tok + 2 * PATCH_MOST
    packed, normed = pl.pallas_call(
        lambda *refs: pack_kernel(heads, tok, *refs),
        out_shape=(shape((per, rows_each, HD)), shape((PATCH_MOST, width))),
        in_specs=[whole] * 8,
        out_specs=(whole, whole),
        compiler_params=vmem(),
        name="pack",
    )(used, gain, proj, query, text_kv, type_bias, d_out, token_types.reshape(tok, 1))
    by_head = lax.all_to_all(packed, "y", 0, 0, tiled=True)
    gathered = lax.all_gather(by_head, "z", axis=0, tiled=True)

    mine = lax.dynamic_slice_in_dim(normed, section * HD, HD, axis=1)
    all_frames = lax.all_to_all(
        jnp.broadcast_to(mine[None], (blocks, PATCH_MOST, HD)), ("z", "y"), 0, 0, tiled=True
    )
    placed = pl.pallas_call(
        lambda *refs: place_kernel(frames, *refs),
        out_shape=shape((group, HD)),
        in_specs=[smem, whole],
        out_specs=whole,
        scratch_shapes=[pltpu.VMEM((group + PATCH_MOST, HD), F32)],
        compiler_params=vmem(),
        name="place",
    )(meta, all_frames)
    norm_pos = lax.all_gather(placed, "phase", axis=0, tiled=False)

    most_chunks = (EPISODE_MOST + group + CHUNK - 2) // CHUNK + 1
    attended, d_query, own_kv, stats = pl.pallas_call(
        lambda *refs: query_kernel(frames, tok, *refs),
        out_shape=(
            shape((group, HD)),
            shape((group, HD)),
            shape((2, group, HD)),
            shape((group // HD, 8, HD), F32),
        ),
        in_specs=[smem, whole, whole],
        out_specs=(whole, whole, whole, whole),
        scratch_shapes=[
            pltpu.VMEM((total + PATCH_MOST, HD), F32),
            pltpu.VMEM((total + PATCH_MOST, HD), F32),
            pltpu.VMEM((total, HD), BF16),
            pltpu.VMEM((total, HD), BF16),
            pltpu.VMEM((group, HD), BF16),
            pltpu.VMEM((group, HD), BF16),
            pltpu.VMEM((most_chunks, group, CHUNK), F32),
            pltpu.VMEM((group, HD), F32),
            pltpu.VMEM((group, HD), F32),
            pltpu.VMEM((group, HD), F32),
        ],
        compiler_params=vmem(),
        name="queries",
    )(meta, start, gathered)
    all_stats = lax.all_to_all(
        jnp.broadcast_to(stats[None], (groups,) + stats.shape), "z", 0, 0, tiled=True
    ).reshape(total // HD, 8, HD)

    d_kv, part = pl.pallas_call(
        lambda *refs: key_kernel(frames, tok, *refs),
        out_shape=(shape((2, group, HD)), shape((sections, HD, 2 * HD))),
        in_specs=[smem, whole, whole, whole, whole, whole],
        out_specs=(whole, whole),
        scratch_shapes=[
            pltpu.VMEM((total, HD), BF16),
            pltpu.VMEM((total, HD), BF16),
            pltpu.VMEM((group, HD), F32),
            pltpu.VMEM((group, HD), F32),
        ],
        compiler_params=vmem(),
        name="keys",
    )(meta, end, gathered, all_stats, own_kv, norm_pos)
    proj_terms = lax.all_to_all(part.reshape(groups, width // groups, 2 * HD), "z", 0, 0, tiled=True)
    proj_rows = width // blocks
    proj_sum = (
        jnp.sum(proj_terms.astype(F32), axis=0)
        .astype(BF16)
        .reshape(per, proj_rows, 2, HD)
        .transpose(0, 2, 1, 3)
        .reshape(per, 2 * proj_rows, HD)
    )
    answers = jnp.concatenate(
        [
            attended.reshape(per, tok, HD),
            d_query.reshape(per, tok, HD),
            d_kv[0].reshape(per, tok, HD),
            d_kv[1].reshape(per, tok, HD),
            proj_sum,
        ],
        axis=1,
    )
    returned = lax.all_to_all(answers, "y", 0, 0, tiled=True)
    att_here, dq_here, d_text_kv, d_proj, terms = pl.pallas_call(
        lambda *refs: unpack_kernel(heads, tok, *refs),
        out_shape=(
            shape((tok, cols)),
            shape((tok, cols)),
            shape((2, tok, cols)),
            shape((proj_rows, 2 * cols), F32),
            shape((sections, tok, width // sections)),
        ),
        in_specs=[whole] * 3,
        out_specs=(whole,) * 5,
        compiler_params=vmem(),
        name="unpack",
    )(returned, is_image, proj)

    summed = lax.all_to_all(terms, "phase", 0, 0, tiled=True)
    routed = pl.pallas_call(
        lambda *refs: route_kernel(frames, tok, *refs),
        out_shape=shape((frames, PATCH_MOST, HD)),
        in_specs=[smem, whole],
        out_specs=whole,
        scratch_shapes=[pltpu.VMEM((tok + PATCH_MOST, HD), F32)],
        compiler_params=vmem(),
        name="route",
    )(meta, summed)
    from_blocks = lax.all_to_all(routed, ("z", "y"), 0, 0, tiled=True)
    source = lax.dynamic_index_in_dim(image_offsets, block, keepdims=False) // tok
    d_slice = lax.dynamic_index_in_dim(from_blocks, source, keepdims=False)
    d_normed = lax.all_gather(d_slice, "phase", axis=0, tiled=False)
    d_patches = pl.pallas_call(
        norm_grad_kernel,
        out_shape=shape(patches.shape),
        in_specs=[whole] * 3,
        out_specs=whole,
        compiler_params=vmem(),
        name="norm_grad",
    )(used, gain, d_normed)
    return (
        att_here,
        dq_here,
        d_text_kv,
        d_proj.reshape(proj_rows, 2, cols),
        d_patches,
    )


def solution(mesh):
    sections, seq = mesh.devices.shape
    per = 4
    inner = Mesh(mesh.devices.reshape(sections, seq // per, per), ("phase", "z", "y"))
    seq = ("z", "y")
    return jax.shard_map(
        shards,
        mesh=inner,
        in_specs=(
            P(seq, None),
            P(),
            P(None, None, "phase"),
            P(seq, "phase"),
            P(None, seq, "phase"),
            P(None, "phase"),
            P(seq, "phase"),
            P(),
            P(),
            P(seq),
            P(),
        ),
        out_specs=(
            P(seq, "phase"),
            P(seq, "phase"),
            P(None, seq, "phase"),
            P(seq, None, "phase"),
            P(seq, None),
        ),
        check_vma=False,
    )
```

```python
import math

import jax
import jax.numpy as jnp
from jax import lax
from jax.experimental import pallas as pl
from jax.experimental.pallas import tpu as pltpu
from jax.sharding import Mesh
from jax.sharding import PartitionSpec as P

HD = 128
PAD = 256
PATCH_MOST = 64
EPISODES = 16
EPISODE_MOST = 2720
EPSILON = 1e-05
NEGATIVE = -1e30
CHUNK = 256

F32 = jnp.float32
BF16 = jnp.bfloat16


def dot_nt(a, b):
    return lax.dot_general(a, b, (((1,), (1,)), ((), ())), preferred_element_type=F32)


def dot_tn(a, b):
    return lax.dot_general(a, b, (((0,), (0,)), ((), ())), preferred_element_type=F32)


def dot_nn(a, b):
    return jnp.dot(a, b, preferred_element_type=F32)


def normalize_rows(patches):
    row_values = patches.astype(F32)
    center = row_values - jnp.mean(row_values, axis=-1, keepdims=True)
    inverse = lax.rsqrt(jnp.mean(center * center, axis=-1, keepdims=True) + EPSILON)
    return (center * inverse, inverse)


def vmem(limit=48):
    return pltpu.CompilerParams(vmem_limit_bytes=limit * 1024 * 1024)


def pack_kernel(heads, tok, patch_ref, gain_ref, proj_ref, q_ref, kv_ref, bias_ref, do_ref, type_ref,
                kv_out, q_out, normed_ref):
    scaled, _ = normalize_rows(patch_ref[...])
    normed = (scaled * gain_ref[...]).astype(BF16)
    normed_ref[...] = normed
    image = dot_nn(normed, proj_ref[...]).astype(BF16)
    cols = heads * HD
    bias = jnp.where(type_ref[...] == 1, bias_ref[1:2].astype(F32), bias_ref[0:1].astype(F32))
    keys = (kv_ref[0].astype(F32) + bias).astype(BF16)
    for h in range(heads):
        span = slice(h * HD, (h + 1) * HD)
        kv_out[h, 0:tok] = keys[:, span]
        kv_out[h, tok : 2 * tok] = kv_ref[1, :, span]
        kv_out[h, 2 * tok : 2 * tok + PATCH_MOST] = image[:, span]
        kv_out[h, 2 * tok + PATCH_MOST :] = image[:, cols + h * HD : cols + (h + 1) * HD]
        q_out[h, 0:tok] = q_ref[:, span]
        q_out[h, tok:] = do_ref[:, span]
    for h in range(heads, kv_out.shape[0]):
        kv_out[h] = jnp.zeros_like(kv_out[h])
        q_out[h] = jnp.zeros_like(q_out[h])


def place_kernel(frames, meta_ref, rows_ref, out_ref, scratch):
    total = out_ref.shape[0]
    scratch[...] = jnp.zeros_like(scratch)
    row = lax.broadcasted_iota(jnp.int32, (PATCH_MOST, HD), 0)

    def one(f, carry):
        where = pl.ds(meta_ref[f], PATCH_MOST)
        live = row < meta_ref[frames + f]
        scratch[where] = jnp.where(live, rows_ref[f].astype(F32), scratch[where])
        return carry

    lax.fori_loop(0, frames, one, 0)

    def low(c, carry):
        where = pl.ds(pl.multiple_of(c * CHUNK, CHUNK), CHUNK)
        out_ref[where] = scratch[where].astype(BF16)
        return carry

    lax.fori_loop(0, total // CHUNK, low, 0)


def query_kernel(frames, tok, meta_ref, start_ref, g_ref, mine_ref, out_ref, own_ref, stat_ref,
                 kf, vf, kb, vb, qb, dob, s_ref, m_ref, l_ref, acc):
    group = own_ref.shape[1]
    total = kb.shape[0]
    scale = 1.0 / math.sqrt(HD)
    power = scale * math.log2(math.e)
    z = meta_ref[2 * frames]
    first_chunk = meta_ref[2 * frames + 2]
    last_chunk = meta_ref[2 * frames + 3]
    image_row = 2 * tok

    def text(b, carry):
        where = pl.ds(pl.multiple_of(b * tok, 32), tok)
        kf[where] = g_ref[b, 0:tok].astype(F32)
        vf[where] = g_ref[b, tok : 2 * tok].astype(F32)
        return carry

    lax.fori_loop(0, total // tok, text, 0)
    row = lax.broadcasted_iota(jnp.int32, (PATCH_MOST, HD), 0)

    def image(f, carry):
        where = pl.ds(meta_ref[f], PATCH_MOST)
        live = row < meta_ref[frames + f]
        kf[where] = jnp.where(live, g_ref[f, image_row : image_row + PATCH_MOST].astype(F32), kf[where])
        vf[where] = jnp.where(live, g_ref[f, image_row + PATCH_MOST :].astype(F32), vf[where])
        return carry

    lax.fori_loop(0, frames, image, 0)

    def low(c, carry):
        where = pl.ds(pl.multiple_of(c * CHUNK, CHUNK), CHUNK)
        kb[where] = kf[where].astype(BF16)
        vb[where] = vf[where].astype(BF16)
        return carry

    lax.fori_loop(0, total // CHUNK, low, 0)
    per = group // tok
    for i in range(per):
        qb[i * tok : (i + 1) * tok] = mine_ref[i, 0:tok]
        dob[i * tok : (i + 1) * tok] = mine_ref[i, tok:]
    own = pl.ds(pl.multiple_of(z * group, HD), group)
    own_ref[0] = kb[own]
    own_ref[1] = vb[own]

    m_ref[...] = jnp.full_like(m_ref, NEGATIVE)
    l_ref[...] = jnp.zeros_like(l_ref)
    acc[...] = jnp.zeros_like(acc)
    lane = lax.broadcasted_iota(jnp.int32, (group, CHUNK), 1)
    query_pos = z * group + lax.broadcasted_iota(jnp.int32, (group, 1), 0)
    start = start_ref[...]

    def chunk(c):
        return pl.ds(pl.multiple_of(c * CHUNK, CHUNK), CHUNK)

    def scores(c, carry):
        s = dot_nt(qb[...], kb[chunk(c)])
        pos = lane + c * CHUNK
        s = jnp.where((pos >= start) & (pos <= query_pos), s, NEGATIVE)
        s_ref[c - first_chunk] = s
        m_ref[...] = jnp.maximum(m_ref[...], jnp.maximum(s[:, :HD], s[:, HD:]))
        return carry

    lax.fori_loop(first_chunk, last_chunk, scores, 0)
    row_max = jnp.max(m_ref[...], axis=1, keepdims=True)
    m_ref[...] = jnp.broadcast_to(row_max, m_ref.shape)

    def weigh(c, carry):
        top = m_ref[...]
        w = jnp.exp2((s_ref[c - first_chunk] - jnp.concatenate([top, top], axis=1)) * power)
        s_ref[c - first_chunk] = w
        l_ref[...] += w[:, :HD] + w[:, HD:]
        acc[...] += dot_nn(w.astype(BF16), vb[chunk(c)])
        return carry

    lax.fori_loop(first_chunk, last_chunk, weigh, 0)
    inverse_sum = 1.0 / jnp.sum(l_ref[...], axis=1, keepdims=True)
    attended = (acc[...] * inverse_sum).astype(BF16)
    for i in range(per):
        out_ref[i, 0:tok] = attended[i * tok : (i + 1) * tok]
    delta = jnp.sum(dob[...].astype(F32) * attended.astype(F32), axis=1, keepdims=True)
    acc[...] = jnp.zeros_like(acc)
    m_ref[...] = jnp.broadcast_to(inverse_sum, m_ref.shape)
    l_ref[...] = jnp.broadcast_to(delta, l_ref.shape)

    def back(c, carry):
        d_prob = dot_nt(dob[...], vb[chunk(c)])
        inv, dlt = m_ref[...], l_ref[...]
        p = s_ref[c - first_chunk] * jnp.concatenate([inv, inv], axis=1)
        d_score = (p * (d_prob - jnp.concatenate([dlt, dlt], axis=1))).astype(BF16)
        acc[...] += dot_nn(d_score, kb[chunk(c)])
        return carry

    lax.fori_loop(first_chunk, last_chunk, back, 0)
    d_query = (acc[...] * scale).astype(BF16)
    for i in range(per):
        out_ref[i, tok:] = d_query[i * tok : (i + 1) * tok]
    which = lax.broadcasted_iota(jnp.int32, (group, HD), 1)
    table = jnp.where(which == 0, row_max, jnp.where(which == 1, inverse_sum, delta))
    for i in range(group // HD):
        stat_ref[i] = jnp.transpose(table[i * HD : (i + 1) * HD])[0:8]


def key_kernel(frames, tok, meta_ref, end_ref, g_ref, stat_ref, own_ref, dkv_ref, out_ref,
               qb, dob, dk, dv):
    group = own_ref.shape[1]
    total = qb.shape[0]
    scale = 1.0 / math.sqrt(HD)
    power = scale * math.log2(math.e)
    z = meta_ref[2 * frames]

    def text(b, carry):
        where = pl.ds(pl.multiple_of(b * tok, 32), tok)
        qb[where] = g_ref[b, 0:tok]
        dob[where] = g_ref[b, tok:]
        return carry

    lax.fori_loop(0, total // tok, text, 0)
    dk[...] = jnp.zeros_like(dk)
    dv[...] = jnp.zeros_like(dv)
    lane = lax.broadcasted_iota(jnp.int32, (group, CHUNK), 1)
    key_pos = z * group + lax.broadcasted_iota(jnp.int32, (group, 1), 0)
    end = end_ref[...]

    def step(c, carry):
        where = pl.ds(pl.multiple_of(c * CHUNK, CHUNK), CHUNK)
        stat = jnp.concatenate([stat_ref[2 * c], stat_ref[2 * c + 1]], axis=1)
        q, do = qb[where], dob[where]
        s = dot_nt(own_ref[0], q)
        pos = lane + c * CHUNK
        p = jnp.exp2((s - stat[0:1]) * power) * stat[1:2]
        p = jnp.where((pos >= key_pos) & (pos < end), p, 0.0)
        dv[...] += dot_nn(p.astype(BF16), do)
        d_prob = dot_nt(own_ref[1], do)
        d_score = (p * (d_prob - stat[2:3])).astype(BF16)
        dk[...] += dot_nn(d_score, q)
        return carry

    lax.fori_loop(meta_ref[2 * frames + 4], meta_ref[2 * frames + 5], step, 0)
    key_grad = (dk[...] * scale).astype(BF16)
    value_grad = dv[...].astype(BF16)
    dkv_ref[:, 0:HD] = key_grad
    dkv_ref[:, HD:] = value_grad
    for i in range(group // tok):
        rows = slice(i * tok, (i + 1) * tok)
        out_ref[i, 0:tok] = key_grad[rows]
        out_ref[i, tok:] = value_grad[rows]


def proj_kernel(norm_ref, grad_ref, out_ref):
    low = dot_tn(norm_ref[...], grad_ref[...]).astype(BF16)
    rows = out_ref.shape[1] // 2
    for i in range(out_ref.shape[0]):
        out_ref[i, 0:rows] = low[i * rows : (i + 1) * rows, 0:HD]
        out_ref[i, rows:] = low[i * rows : (i + 1) * rows, HD:]


def unpack_queries_kernel(heads, tok, r_ref, att_ref, dq_ref):
    for h in range(heads):
        span = slice(h * HD, (h + 1) * HD)
        att_ref[:, span] = r_ref[h, 0:tok]
        dq_ref[:, span] = r_ref[h, tok:]


def unpack_kernel(heads, tok, r_ref, image_ref, proj_ref, dtext_ref, dn_ref):
    is_image = image_ref[...] == 1
    parts = [None] * (2 * heads)
    for h in range(heads):
        span = slice(h * HD, (h + 1) * HD)
        for c in range(2):
            grad = r_ref[h, c * tok : (c + 1) * tok]
            zero = jnp.zeros_like(grad)
            dtext_ref[c, :, span] = jnp.where(is_image, zero, grad)
            parts[c * heads + h] = jnp.where(is_image, grad, zero)
    grads = jnp.concatenate(parts, axis=1)
    for i in range(dn_ref.shape[0]):
        dn_ref[i] = dot_nt(grads, proj_ref[i * HD : (i + 1) * HD]).astype(BF16)


def route_kernel(frames, tok, meta_ref, dn_ref, out_ref, scratch):
    first = meta_ref[2 * frames + 1] * tok
    total = dn_ref[0].astype(F32)
    for i in range(1, dn_ref.shape[0]):
        total = total + dn_ref[i].astype(F32)
    scratch[...] = jnp.zeros_like(scratch)
    scratch[0:tok] = total
    row = lax.broadcasted_iota(jnp.int32, (PATCH_MOST, HD), 0)

    def one(f, carry):
        offset = meta_ref[f] - first
        here = (offset >= 0) & (offset < tok)
        live = jnp.where(here, meta_ref[frames + f], 0)
        rows = scratch[pl.ds(jnp.where(here, offset, 0), PATCH_MOST)]
        out_ref[f] = jnp.where(row < live, rows, 0.0).astype(BF16)
        return carry

    lax.fori_loop(0, frames, one, 0)


def norm_grad_kernel(patch_ref, gain_ref, dn_ref, out_ref):
    scaled, inverse = normalize_rows(patch_ref[...])
    d_normed = jnp.concatenate([dn_ref[i] for i in range(dn_ref.shape[0])], axis=1).astype(F32)
    scaled_grad = d_normed * gain_ref[...]
    d_rows = (
        scaled_grad
        - jnp.mean(scaled_grad, axis=-1, keepdims=True)
        - scaled * jnp.mean(scaled_grad * scaled, axis=-1, keepdims=True)
    ) * inverse
    out_ref[0:PATCH_MOST] = d_rows.astype(BF16)
    out_ref[PATCH_MOST:] = jnp.zeros((out_ref.shape[0] - PATCH_MOST, out_ref.shape[1]), BF16)


def shards(patches, ln_gain, kv_proj, query, text_kv, type_bias, d_out, patch_counts, image_offsets,
           token_types, segment_ids):
    tok, cols = query.shape
    heads = cols // HD
    width = patches.shape[1]
    groups, per, sections = lax.axis_size("z"), lax.axis_size("y"), lax.axis_size("phase")
    frames = patch_counts.shape[0]
    blocks = groups * per
    group = per * tok
    total = blocks * tok
    z, y, section = lax.axis_index("z"), lax.axis_index("y"), lax.axis_index("phase")
    block = z * per + y
    smem = pl.BlockSpec(memory_space=pltpu.SMEM)
    whole = pl.BlockSpec(memory_space=pltpu.VMEM)

    def shape(dims, kind=BF16):
        return jax.ShapeDtypeStruct(dims, kind)

    ids = jnp.arange(EPISODES, dtype=jnp.int32)
    seg_first = jnp.sum((segment_ids[None, :] < ids[:, None]).astype(jnp.int32), axis=1)
    seg_end = jnp.sum((segment_ids[None, :] <= ids[:, None]).astype(jnp.int32), axis=1)
    own_seg = lax.dynamic_slice_in_dim(segment_ids, z * group, group)
    same = own_seg[:, None] == ids[None, :]
    start = jnp.sum(jnp.where(same, seg_first[None, :], 0), axis=1, keepdims=True)
    end = jnp.sum(jnp.where(same, seg_end[None, :], 0), axis=1, keepdims=True)
    scalars = jnp.stack([
        z,
        block,
        start[0, 0] // CHUNK,
        ((z + 1) * group + CHUNK - 1) // CHUNK,
        (z * group) // CHUNK,
        (end[group - 1, 0] + CHUNK - 1) // CHUNK,
    ]).astype(jnp.int32)
    meta = jnp.concatenate([image_offsets, patch_counts, scalars])
    positions = block * tok + jnp.arange(tok, dtype=jnp.int32)
    is_image = jnp.any(
        (positions[:, None] >= image_offsets[None, :])
        & (positions[:, None] < image_offsets[None, :] + patch_counts[None, :]),
        axis=1, keepdims=True,
    ).astype(jnp.int32)

    gain = ln_gain.reshape(1, width)
    proj = kv_proj.reshape(width, 2 * cols)
    used = patches[:PATCH_MOST]
    packed, questions, normed = pl.pallas_call(
        lambda *refs: pack_kernel(heads, tok, *refs),
        out_shape=(
            shape((per, 2 * tok + 2 * PATCH_MOST, HD)),
            shape((per, 2 * tok, HD)),
            shape((PATCH_MOST, width)),
        ),
        in_specs=[whole] * 8,
        out_specs=(whole, whole, whole),
        compiler_params=vmem(),
        name="pack",
    )(used, gain, proj, query, text_kv, type_bias, d_out, token_types.reshape(tok, 1))
    kv_mine = lax.all_to_all(packed, "y", 0, 0, tiled=True)
    kv_all = lax.all_gather(kv_mine, "z", axis=0, tiled=True)
    questions, _ = lax.optimization_barrier((questions, kv_mine))
    q_mine = lax.all_to_all(questions, "y", 0, 0, tiled=True)
    q_all = lax.all_gather(q_mine, "z", axis=0, tiled=True)

    normed, _ = lax.optimization_barrier((normed, q_mine))
    slices = normed.reshape(PATCH_MOST, groups, 1, HD).transpose(1, 2, 0, 3)
    all_frames = lax.all_to_all(
        jnp.broadcast_to(slices, (groups, per, PATCH_MOST, HD)).reshape(blocks, PATCH_MOST, HD),
        ("z", "y"), 0, 0, tiled=True,
    )
    norm_pos = pl.pallas_call(
        lambda *refs: place_kernel(frames, *refs),
        out_shape=shape((total, HD)),
        in_specs=[smem, whole],
        out_specs=whole,
        scratch_shapes=[pltpu.VMEM((total + PATCH_MOST, HD), F32)],
        compiler_params=vmem(),
        name="place",
    )(meta, all_frames)
    kv_all, norm_pos = lax.optimization_barrier((kv_all, norm_pos))

    most_chunks = (EPISODE_MOST + group + CHUNK - 2) // CHUNK + 1
    answers, own_kv, stats = pl.pallas_call(
        lambda *refs: query_kernel(frames, tok, *refs),
        out_shape=(
            shape((per, 2 * tok, HD)),
            shape((2, group, HD)),
            shape((group // HD, 8, HD), F32),
        ),
        in_specs=[smem, whole, whole, whole],
        out_specs=(whole, whole, whole),
        scratch_shapes=[
            pltpu.VMEM((total + PATCH_MOST, HD), F32),
            pltpu.VMEM((total + PATCH_MOST, HD), F32),
            pltpu.VMEM((total, HD), BF16),
            pltpu.VMEM((total, HD), BF16),
            pltpu.VMEM((group, HD), BF16),
            pltpu.VMEM((group, HD), BF16),
            pltpu.VMEM((most_chunks, group, CHUNK), F32),
            pltpu.VMEM((group, HD), F32),
            pltpu.VMEM((group, HD), F32),
            pltpu.VMEM((group, HD), F32),
        ],
        compiler_params=vmem(),
        name="queries",
    )(meta, start, kv_all, q_mine)
    all_stats = lax.all_to_all(
        jnp.broadcast_to(stats[None], (groups,) + stats.shape), "z", 0, 0, tiled=True
    ).reshape(total // HD, 8, HD)
    answers, all_stats = lax.optimization_barrier((answers, all_stats))
    returned = lax.all_to_all(answers, "y", 0, 0, tiled=True)
    att_here, dq_here = pl.pallas_call(
        lambda *refs: unpack_queries_kernel(heads, tok, *refs),
        out_shape=(shape((tok, cols)), shape((tok, cols))),
        in_specs=[whole],
        out_specs=(whole, whole),
        compiler_params=vmem(),
        name="unpack_queries",
    )(returned)
    q_all, returned = lax.optimization_barrier((q_all, returned))

    d_kv, key_grads = pl.pallas_call(
        lambda *refs: key_kernel(frames, tok, *refs),
        out_shape=(shape((group, 2 * HD)), shape((per, 2 * tok, HD))),
        in_specs=[smem] + [whole] * 4,
        out_specs=(whole, whole),
        scratch_shapes=[
            pltpu.VMEM((total, HD), BF16),
            pltpu.VMEM((total, HD), BF16),
            pltpu.VMEM((group, HD), F32),
            pltpu.VMEM((group, HD), F32),
        ],
        compiler_params=vmem(),
        name="keys",
    )(meta, end, q_all, all_stats, own_kv)
    d_kv_all = lax.all_gather(d_kv, "z", axis=0, tiled=True)
    keys_back = lax.all_to_all(key_grads, "y", 0, 0, tiled=True)
    d_text_kv, terms = pl.pallas_call(
        lambda *refs: unpack_kernel(heads, tok, *refs),
        out_shape=(shape((2, tok, cols)), shape((sections, tok, width // sections))),
        in_specs=[whole] * 3,
        out_specs=(whole,) * 2,
        compiler_params=vmem(),
        name="unpack",
    )(keys_back, is_image, proj)

    summed = lax.all_to_all(terms, "phase", 0, 0, tiled=True)
    routed = pl.pallas_call(
        lambda *refs: route_kernel(frames, tok, *refs),
        out_shape=shape((frames, PATCH_MOST, HD)),
        in_specs=[smem, whole],
        out_specs=whole,
        scratch_shapes=[pltpu.VMEM((tok + PATCH_MOST, HD), F32)],
        compiler_params=vmem(),
        name="route",
    )(meta, summed)
    from_blocks = lax.all_to_all(routed, ("z", "y"), 0, 0, tiled=True)
    source = lax.dynamic_index_in_dim(image_offsets, block, keepdims=False) // tok
    d_slice = lax.dynamic_index_in_dim(from_blocks, source, keepdims=False)
    d_normed = lax.all_to_all(
        jnp.broadcast_to(d_slice[None], (sections,) + d_slice.shape), "phase", 0, 0, tiled=True
    )
    proj_rows = width // blocks
    proj_head = pl.pallas_call(
        proj_kernel,
        out_shape=shape((per, 2 * proj_rows, HD)),
        in_specs=[whole] * 2,
        out_specs=whole,
        compiler_params=vmem(),
        name="proj_grad",
    )(norm_pos, d_kv_all)
    proj_back = lax.all_to_all(proj_head, "y", 0, 0, tiled=True)
    d_proj = (
        proj_back[:heads].astype(F32)
        .reshape(heads, 2, proj_rows, HD)
        .transpose(2, 1, 0, 3)
        .reshape(proj_rows, 2, cols)
    )
    d_patches = pl.pallas_call(
        norm_grad_kernel,
        out_shape=shape(patches.shape),
        in_specs=[whole] * 3,
        out_specs=whole,
        compiler_params=vmem(),
        name="norm_grad",
    )(used, gain, d_normed)
    return (
        att_here,
        dq_here,
        d_text_kv,
        d_proj,
        d_patches,
    )


def solution(mesh):
    sections, seq = mesh.devices.shape
    per = 4
    inner = Mesh(mesh.devices.reshape(sections, seq // per, per), ("phase", "z", "y"))
    seq = ("z", "y")
    return jax.shard_map(
        shards,
        mesh=inner,
        in_specs=(
            P(seq, None),
            P(),
            P(None, None, "phase"),
            P(seq, "phase"),
            P(None, seq, "phase"),
            P(None, "phase"),
            P(seq, "phase"),
            P(),
            P(),
            P(seq),
            P(),
        ),
        out_specs=(
            P(seq, "phase"),
            P(seq, "phase"),
            P(None, seq, "phase"),
            P(seq, None, "phase"),
            P(seq, None),
        ),
        check_vma=False,
    )
```

```python
import math

import jax
import jax.numpy as jnp
from jax import lax
from jax.experimental import pallas as pl
from jax.experimental.pallas import tpu as pltpu
from jax.sharding import Mesh
from jax.sharding import PartitionSpec as P

HD = 128
PAD = 256
PATCH_MOST = 64
EPISODES = 16
EPISODE_MOST = 2720
EPSILON = 1e-05
NEGATIVE = -1e30
CHUNK = 256
STAT_ROWS = 16

F32 = jnp.float32
BF16 = jnp.bfloat16


def dot_nt(a, b):
    return lax.dot_general(a, b, (((1,), (1,)), ((), ())), preferred_element_type=F32)


def dot_tn(a, b):
    return lax.dot_general(a, b, (((0,), (0,)), ((), ())), preferred_element_type=F32)


def dot_nn(a, b):
    return jnp.dot(a, b, preferred_element_type=F32)


def normalize_rows(patches):
    row_values = patches.astype(F32)
    center = row_values - jnp.mean(row_values, axis=-1, keepdims=True)
    inverse = lax.rsqrt(jnp.mean(center * center, axis=-1, keepdims=True) + EPSILON)
    return (center * inverse, inverse)


def vmem(limit=48):
    return pltpu.CompilerParams(vmem_limit_bytes=limit * 1024 * 1024)


def pack_kernel(heads, tok, patch_ref, gain_ref, proj_ref, q_ref, kv_ref, bias_ref, do_ref, type_ref,
                kv_out, q_out, normed_ref):
    scaled, _ = normalize_rows(patch_ref[0:PATCH_MOST])
    normed = (scaled * gain_ref[...]).astype(BF16)
    for i in range(normed_ref.shape[0]):
        normed_ref[i] = normed[:, i * HD : (i + 1) * HD]
    image = dot_nn(normed, proj_ref[...]).astype(BF16)
    cols = heads * HD
    bias = jnp.where(type_ref[...] == 1, bias_ref[1:2].astype(F32), bias_ref[0:1].astype(F32))
    keys = (kv_ref[0].astype(F32) + bias).astype(BF16)
    for h in range(heads):
        span = slice(h * HD, (h + 1) * HD)
        kv_out[h, 0:tok] = keys[:, span]
        kv_out[h, tok : 2 * tok] = kv_ref[1, :, span]
        kv_out[h, 2 * tok : 2 * tok + PATCH_MOST] = image[:, span]
        kv_out[h, 2 * tok + PATCH_MOST :] = image[:, cols + h * HD : cols + (h + 1) * HD]
        q_out[h, 0:tok] = q_ref[:, span]
        q_out[h, tok:] = do_ref[:, span]
    for h in range(heads, kv_out.shape[0]):
        kv_out[h] = jnp.zeros_like(kv_out[h])
        q_out[h] = jnp.zeros_like(q_out[h])


def place_kernel(frames, meta_ref, rows_ref, out_ref, scratch):
    total = out_ref.shape[0]
    per = rows_ref.shape[0]
    scratch[...] = jnp.zeros_like(scratch)
    row = lax.broadcasted_iota(jnp.int32, (PATCH_MOST, HD), 0)

    def one(f, carry):
        where = pl.ds(meta_ref[f], PATCH_MOST)
        live = row < meta_ref[frames + f]
        rows = rows_ref[lax.rem(f, per), lax.div(f, per)].astype(F32)
        scratch[where] = jnp.where(live, rows, scratch[where])
        return carry

    lax.fori_loop(0, frames, one, 0)

    def low(c, carry):
        where = pl.ds(pl.multiple_of(c * CHUNK, CHUNK), CHUNK)
        out_ref[where] = scratch[where].astype(BF16)
        return carry

    lax.fori_loop(0, total // CHUNK, low, 0)


def query_kernel(frames, tok, meta_ref, start_ref, g_ref, mine_ref, out_hbm, own_hbm, stat_hbm,
                 out_ref, own_ref, stat_ref, out_sem, kf, vf, kb, vb, qb, dob, s_ref, m_ref, l_ref, acc):
    group = own_ref.shape[1]
    total = kb.shape[0]
    scale = 1.0 / math.sqrt(HD)
    power = scale * math.log2(math.e)
    z = meta_ref[2 * frames]
    first_chunk = meta_ref[2 * frames + 2]
    last_chunk = meta_ref[2 * frames + 3]
    image_row = 2 * tok

    def text(b, carry):
        where = pl.ds(pl.multiple_of(b * tok, 32), tok)
        kf[where] = g_ref[b, 0:tok].astype(F32)
        vf[where] = g_ref[b, tok : 2 * tok].astype(F32)
        return carry

    lax.fori_loop(0, total // tok, text, 0)
    row = lax.broadcasted_iota(jnp.int32, (PATCH_MOST, HD), 0)

    def image(f, carry):
        where = pl.ds(meta_ref[f], PATCH_MOST)
        live = row < meta_ref[frames + f]
        kf[where] = jnp.where(live, g_ref[f, image_row : image_row + PATCH_MOST].astype(F32), kf[where])
        vf[where] = jnp.where(live, g_ref[f, image_row + PATCH_MOST :].astype(F32), vf[where])
        return carry

    lax.fori_loop(0, frames, image, 0)

    def low(c, carry):
        where = pl.ds(pl.multiple_of(c * CHUNK, CHUNK), CHUNK)
        kb[where] = kf[where].astype(BF16)
        vb[where] = vf[where].astype(BF16)
        return carry

    lax.fori_loop(0, total // CHUNK, low, 0)
    per = group // tok
    for i in range(per):
        qb[i * tok : (i + 1) * tok] = mine_ref[i, 0:tok]
        dob[i * tok : (i + 1) * tok] = mine_ref[i, tok:]
    own = pl.ds(pl.multiple_of(z * group, HD), group)
    own_ref[0] = kb[own]
    own_ref[1] = vb[own]
    own_copy = pltpu.make_async_copy(own_ref, own_hbm, out_sem.at[0])
    own_copy.start()

    m_ref[...] = jnp.full_like(m_ref, NEGATIVE)
    l_ref[...] = jnp.zeros_like(l_ref)
    acc[...] = jnp.zeros_like(acc)
    lane = lax.broadcasted_iota(jnp.int32, (group, CHUNK), 1)
    query_pos = z * group + lax.broadcasted_iota(jnp.int32, (group, 1), 0)
    start = start_ref[...]

    def chunk(c):
        return pl.ds(pl.multiple_of(c * CHUNK, CHUNK), CHUNK)

    def scores(c, carry):
        s = dot_nt(qb[...], kb[chunk(c)])
        pos = lane + c * CHUNK
        s = jnp.where((pos >= start) & (pos <= query_pos), s, NEGATIVE)
        s_ref[c - first_chunk] = s
        m_ref[...] = jnp.maximum(m_ref[...], jnp.maximum(s[:, :HD], s[:, HD:]))
        return carry

    lax.fori_loop(first_chunk, last_chunk, scores, 0)
    row_max = jnp.max(m_ref[...], axis=1, keepdims=True)
    m_ref[...] = jnp.broadcast_to(row_max, m_ref.shape)

    def weigh(c, carry):
        top = m_ref[...]
        w = jnp.exp2((s_ref[c - first_chunk] - jnp.concatenate([top, top], axis=1)) * power)
        s_ref[c - first_chunk] = w
        l_ref[...] += w[:, :HD] + w[:, HD:]
        acc[...] += dot_nn(w.astype(BF16), vb[chunk(c)])
        return carry

    lax.fori_loop(first_chunk, last_chunk, weigh, 0)
    inverse_sum = 1.0 / jnp.sum(l_ref[...], axis=1, keepdims=True)
    attended = (acc[...] * inverse_sum).astype(BF16)
    for i in range(per):
        out_ref[i, 0:tok] = attended[i * tok : (i + 1) * tok]
    delta = jnp.sum(dob[...].astype(F32) * attended.astype(F32), axis=1, keepdims=True)
    acc[...] = jnp.zeros_like(acc)
    m_ref[...] = jnp.broadcast_to(inverse_sum, m_ref.shape)
    l_ref[...] = jnp.broadcast_to(delta, l_ref.shape)

    def back(c, carry):
        d_prob = dot_nt(dob[...], vb[chunk(c)])
        inv, dlt = m_ref[...], l_ref[...]
        p = s_ref[c - first_chunk] * jnp.concatenate([inv, inv], axis=1)
        d_score = (p * (d_prob - jnp.concatenate([dlt, dlt], axis=1))).astype(BF16)
        acc[...] += dot_nn(d_score, kb[chunk(c)])
        return carry

    lax.fori_loop(first_chunk, last_chunk, back, 0)
    d_query = (acc[...] * scale).astype(BF16)
    for i in range(per):
        out_ref[i, tok:] = d_query[i * tok : (i + 1) * tok]
    which = lax.broadcasted_iota(jnp.int32, (group, HD), 1)
    table = jnp.where(which == 0, row_max, jnp.where(which == 1, inverse_sum, delta))
    tiles = [jnp.transpose(table[i * HD : (i + 1) * HD])[0:8] for i in range(group // HD)]
    stat = jnp.concatenate([t[k : k + 1] for k in range(3) for t in tiles], axis=0)
    stat = jnp.concatenate([stat, stat[0:1]], axis=0)
    for i in range(stat_ref.shape[0]):
        stat_ref[i] = stat
    stat_copy = pltpu.make_async_copy(stat_ref, stat_hbm, out_sem.at[1])
    out_copy = pltpu.make_async_copy(out_ref, out_hbm, out_sem.at[2])
    stat_copy.start()
    out_copy.start()
    own_copy.wait()
    stat_copy.wait()
    out_copy.wait()


def key_kernel(frames, tok, meta_ref, end_ref, g_hbm, stat_hbm, own_hbm, dkv_hbm, out_hbm,
               qb, dob, stat_ref, own_ref, dk, dv, rows_ref, out_ref, q_sem, do_sem, in_sem, out_sem):
    group = own_ref.shape[1]
    per = group // tok
    scale = 1.0 / math.sqrt(HD)
    power = scale * math.log2(math.e)
    z = meta_ref[2 * frames]
    count = meta_ref[2 * frames + 5]
    last_tile = stat_ref.shape[0] * (group // HD) - 1

    def fetch(i):
        where = pl.ds(pl.multiple_of(i * tok, 32), tok)
        b = z * per + i
        return (
            pltpu.make_async_copy(g_hbm.at[b, 0:tok], qb.at[where], q_sem.at[i]),
            pltpu.make_async_copy(g_hbm.at[b, tok : 2 * tok], dob.at[where], do_sem.at[i]),
        )

    own_copy = pltpu.make_async_copy(own_hbm, own_ref, in_sem.at[0])
    stat_copy = pltpu.make_async_copy(stat_hbm, stat_ref, in_sem.at[1])
    own_copy.start()
    stat_copy.start()

    def begin(i, carry):
        for copy in fetch(i):
            copy.start()
        return carry

    def finish(i, carry):
        for copy in fetch(i):
            copy.wait()
        return carry

    lax.fori_loop(0, count, begin, 0)
    dk[...] = jnp.zeros_like(dk)
    dv[...] = jnp.zeros_like(dv)
    tail = pl.ds(pl.multiple_of(count * tok, 32), CHUNK)
    qb[tail] = jnp.zeros((CHUNK, HD), BF16)
    dob[tail] = jnp.zeros((CHUNK, HD), BF16)
    lane = lax.broadcasted_iota(jnp.int32, (group, CHUNK), 1)
    key_pos = lax.broadcasted_iota(jnp.int32, (group, 1), 0)
    end = end_ref[...] - z * group
    own_copy.wait()
    stat_copy.wait()

    def statistics(c, kind):
        parts = []
        for half in range(2):
            tile = jnp.minimum(z * (group // HD) + 2 * c + half, last_tile)
            at = lax.div(tile, group // HD)
            row = kind * (group // HD) + lax.rem(tile, group // HD)
            parts.append(stat_ref[at, pl.ds(row, 1)])
        return jnp.concatenate(parts, axis=1)

    def step(c, carry):
        where = pl.ds(pl.multiple_of(c * CHUNK, CHUNK), CHUNK)
        arrived = lax.div(c * CHUNK + tok - 1, tok)
        needed = jnp.minimum(lax.div((c + 1) * CHUNK + tok - 1, tok), count)
        lax.fori_loop(arrived, needed, finish, 0)
        q, do = qb[where], dob[where]
        s = dot_nt(own_ref[0], q)
        pos = lane + c * CHUNK
        p = jnp.exp2((s - statistics(c, 0)) * power) * statistics(c, 1)
        p = jnp.where((pos >= key_pos) & (pos < end), p, 0.0)
        dv[...] += dot_nn(p.astype(BF16), do)
        d_prob = dot_nt(own_ref[1], do)
        d_score = (p * (d_prob - statistics(c, 2))).astype(BF16)
        dk[...] += dot_nn(d_score, q)
        return carry

    lax.fori_loop(0, meta_ref[2 * frames + 4], step, 0)
    key_grad = (dk[...] * scale).astype(BF16)
    value_grad = dv[...].astype(BF16)
    rows_ref[:, 0:HD] = key_grad
    rows_ref[:, HD:] = value_grad
    rows_copy = pltpu.make_async_copy(rows_ref, dkv_hbm, out_sem.at[0])
    rows_copy.start()
    for i in range(per):
        rows = slice(i * tok, (i + 1) * tok)
        out_ref[i, 0:tok] = key_grad[rows]
        out_ref[i, tok:] = value_grad[rows]
    out_copy = pltpu.make_async_copy(out_ref, out_hbm, out_sem.at[1])
    out_copy.start()
    rows_copy.wait()
    out_copy.wait()


def proj_kernel(norm_ref, grad_ref, out_ref):
    low = dot_tn(norm_ref[...], grad_ref[...]).astype(BF16)
    rows = out_ref.shape[1] // 2
    for i in range(out_ref.shape[0]):
        out_ref[i, 0:rows] = low[i * rows : (i + 1) * rows, 0:HD]
        out_ref[i, rows:] = low[i * rows : (i + 1) * rows, HD:]


def unpack_queries_kernel(heads, tok, r_ref, att_ref, dq_ref):
    for h in range(heads):
        span = slice(h * HD, (h + 1) * HD)
        att_ref[:, span] = r_ref[h, 0:tok]
        dq_ref[:, span] = r_ref[h, tok:]


def unpack_kernel(heads, tok, meta_ref, offset_ref, count_ref, r_ref, proj_ref, dtext_ref, dn_ref):
    frames = offset_ref.shape[1]
    pos = meta_ref[2 * frames + 1] * tok + lax.broadcasted_iota(jnp.int32, (tok, frames), 0)
    begin = offset_ref[...]
    inside = (pos >= begin) & (pos < begin + count_ref[...])
    is_image = jnp.max(inside.astype(F32), axis=1, keepdims=True) > 0.5
    parts = [None] * (2 * heads)
    for h in range(heads):
        span = slice(h * HD, (h + 1) * HD)
        for c in range(2):
            grad = r_ref[h, c * tok : (c + 1) * tok]
            zero = jnp.zeros_like(grad)
            dtext_ref[c, :, span] = jnp.where(is_image, zero, grad)
            parts[c * heads + h] = jnp.where(is_image, grad, zero)
    grads = jnp.concatenate(parts, axis=1)
    for i in range(dn_ref.shape[0]):
        dn_ref[i] = dot_nt(grads, proj_ref[i * HD : (i + 1) * HD]).astype(BF16)


def route_kernel(frames, tok, meta_ref, dn_ref, out_ref, scratch):
    first = meta_ref[2 * frames + 1] * tok
    total = dn_ref[0].astype(F32)
    for i in range(1, dn_ref.shape[0]):
        total = total + dn_ref[i].astype(F32)
    scratch[...] = jnp.zeros_like(scratch)
    scratch[0:tok] = total
    row = lax.broadcasted_iota(jnp.int32, (PATCH_MOST, HD), 0)

    def one(f, carry):
        offset = meta_ref[f] - first
        here = (offset >= 0) & (offset < tok)
        live = jnp.where(here, meta_ref[frames + f], 0)
        rows = scratch[pl.ds(jnp.where(here, offset, 0), PATCH_MOST)]
        out_ref[f] = jnp.where(row < live, rows, 0.0).astype(BF16)
        return carry

    lax.fori_loop(0, frames, one, 0)


def norm_grad_kernel(patch_ref, gain_ref, dn_ref, out_ref):
    scaled, inverse = normalize_rows(patch_ref[0:PATCH_MOST])
    d_normed = jnp.concatenate([dn_ref[i] for i in range(dn_ref.shape[0])], axis=1).astype(F32)
    scaled_grad = d_normed * gain_ref[...]
    d_rows = (
        scaled_grad
        - jnp.mean(scaled_grad, axis=-1, keepdims=True)
        - scaled * jnp.mean(scaled_grad * scaled, axis=-1, keepdims=True)
    ) * inverse
    out_ref[0:PATCH_MOST] = d_rows.astype(BF16)
    out_ref[PATCH_MOST:] = jnp.zeros((out_ref.shape[0] - PATCH_MOST, out_ref.shape[1]), BF16)


def shards(patches, ln_gain, kv_proj, query, text_kv, type_bias, d_out, patch_counts, image_offsets,
           token_types, segment_ids):
    tok, cols = query.shape
    heads = cols // HD
    width = patches.shape[1]
    groups, per, sections = lax.axis_size("z"), lax.axis_size("y"), lax.axis_size("phase")
    frames = patch_counts.shape[0]
    blocks = groups * per
    group = per * tok
    total = blocks * tok
    z, y, section = lax.axis_index("z"), lax.axis_index("y"), lax.axis_index("phase")
    block = z * per + y
    smem = pl.BlockSpec(memory_space=pltpu.SMEM)
    whole = pl.BlockSpec(memory_space=pltpu.VMEM)
    hbm = pl.BlockSpec(memory_space=pltpu.HBM)

    def shape(dims, kind=BF16):
        return jax.ShapeDtypeStruct(dims, kind)

    ids = jnp.arange(EPISODES, dtype=jnp.int32)
    seg_first = jnp.sum((segment_ids[None, :] < ids[:, None]).astype(jnp.int32), axis=1)
    seg_end = jnp.sum((segment_ids[None, :] <= ids[:, None]).astype(jnp.int32), axis=1)
    own_seg = lax.dynamic_slice_in_dim(segment_ids, z * group, group)
    same = own_seg[:, None] == ids[None, :]
    start = jnp.sum(jnp.where(same, seg_first[None, :], 0), axis=1, keepdims=True)
    end = jnp.sum(jnp.where(same, seg_end[None, :], 0), axis=1, keepdims=True)
    scalars = jnp.stack([
        z,
        block,
        start[0, 0] // CHUNK,
        ((z + 1) * group + CHUNK - 1) // CHUNK,
        (end[group - 1, 0] - z * group + CHUNK - 1) // CHUNK,
        (end[group - 1, 0] - z * group + tok - 1) // tok,
    ]).astype(jnp.int32)
    meta = jnp.concatenate([image_offsets, patch_counts, scalars])
    gain = ln_gain.reshape(1, width)
    proj = kv_proj.reshape(width, 2 * cols)
    packed, questions, normed = pl.pallas_call(
        lambda *refs: pack_kernel(heads, tok, *refs),
        out_shape=(
            shape((per, 2 * tok + 2 * PATCH_MOST, HD)),
            shape((per, 2 * tok, HD)),
            shape((groups, PATCH_MOST, HD)),
        ),
        in_specs=[whole] * 8,
        out_specs=(whole, whole, whole),
        compiler_params=vmem(),
        name="pack",
    )(patches, gain, proj, query, text_kv, type_bias, d_out, token_types.reshape(tok, 1))
    kv_mine = lax.all_to_all(packed, "y", 0, 0, tiled=True)
    kv_all = lax.all_gather(kv_mine, "z", axis=0, tiled=True)
    questions, _ = lax.optimization_barrier((questions, kv_mine))
    q_mine = lax.all_to_all(questions, "y", 0, 0, tiled=True)
    q_all = lax.all_gather(q_mine, "z", axis=0, tiled=True)

    normed, _ = lax.optimization_barrier((normed, q_mine))
    some_frames = lax.all_to_all(normed, "z", 0, 0, tiled=True)
    all_frames = lax.all_gather(some_frames, "y", axis=0, tiled=False)
    norm_pos = pl.pallas_call(
        lambda *refs: place_kernel(frames, *refs),
        out_shape=shape((total, HD)),
        in_specs=[smem, whole],
        out_specs=whole,
        scratch_shapes=[pltpu.VMEM((total + PATCH_MOST, HD), F32)],
        compiler_params=vmem(),
        name="place",
    )(meta, all_frames)
    kv_all, norm_pos = lax.optimization_barrier((kv_all, norm_pos))

    most_blocks = (group - 1 + EPISODE_MOST + tok - 1) // tok
    most_chunks = (EPISODE_MOST + group + CHUNK - 2) // CHUNK + 1
    answers, own_kv, stats = pl.pallas_call(
        lambda *refs: query_kernel(frames, tok, *refs),
        out_shape=(
            shape((per, 2 * tok, HD)),
            shape((2, group, HD)),
            shape((groups, STAT_ROWS, HD), F32),
        ),
        in_specs=[smem, whole, whole, whole],
        out_specs=(hbm, hbm, hbm),
        scratch_shapes=[
            pltpu.VMEM((per, 2 * tok, HD), BF16),
            pltpu.VMEM((2, group, HD), BF16),
            pltpu.VMEM((groups, STAT_ROWS, HD), F32),
            pltpu.SemaphoreType.DMA((3,)),
            pltpu.VMEM((total + PATCH_MOST, HD), F32),
            pltpu.VMEM((total + PATCH_MOST, HD), F32),
            pltpu.VMEM((total, HD), BF16),
            pltpu.VMEM((total, HD), BF16),
            pltpu.VMEM((group, HD), BF16),
            pltpu.VMEM((group, HD), BF16),
            pltpu.VMEM((most_chunks, group, CHUNK), F32),
            pltpu.VMEM((group, HD), F32),
            pltpu.VMEM((group, HD), F32),
            pltpu.VMEM((group, HD), F32),
        ],
        compiler_params=vmem(62),
        name="queries",
    )(meta, start, kv_all, q_mine)
    all_stats = lax.all_to_all(stats, "z", 0, 0, tiled=True)
    answers, all_stats = lax.optimization_barrier((answers, all_stats))
    returned = lax.all_to_all(answers, "y", 0, 0, tiled=True)
    att_here, dq_here = pl.pallas_call(
        lambda *refs: unpack_queries_kernel(heads, tok, *refs),
        out_shape=(shape((tok, cols)), shape((tok, cols))),
        in_specs=[whole],
        out_specs=(whole, whole),
        compiler_params=vmem(),
        name="unpack_queries",
    )(returned)
    q_all, returned = lax.optimization_barrier((q_all, returned))

    d_kv, key_grads = pl.pallas_call(
        lambda *refs: key_kernel(frames, tok, *refs),
        out_shape=(shape((group, 2 * HD)), shape((per, 2 * tok, HD))),
        in_specs=[smem, whole, hbm, hbm, hbm],
        out_specs=(hbm, hbm),
        scratch_shapes=[
            pltpu.VMEM((most_blocks * tok + CHUNK, HD), BF16),
            pltpu.VMEM((most_blocks * tok + CHUNK, HD), BF16),
            pltpu.VMEM((groups, STAT_ROWS, HD), F32),
            pltpu.VMEM((2, group, HD), BF16),
            pltpu.VMEM((group, HD), F32),
            pltpu.VMEM((group, HD), F32),
            pltpu.VMEM((group, 2 * HD), BF16),
            pltpu.VMEM((per, 2 * tok, HD), BF16),
            pltpu.SemaphoreType.DMA((most_blocks,)),
            pltpu.SemaphoreType.DMA((most_blocks,)),
            pltpu.SemaphoreType.DMA((2,)),
            pltpu.SemaphoreType.DMA((2,)),
        ],
        compiler_params=vmem(62),
        name="keys",
    )(meta, end, q_all, all_stats, own_kv)
    d_kv_all = lax.all_gather(d_kv, "z", axis=0, tiled=True)
    keys_back = lax.all_to_all(key_grads, "y", 0, 0, tiled=True)
    d_text_kv, terms = pl.pallas_call(
        lambda *refs: unpack_kernel(heads, tok, *refs),
        out_shape=(shape((2, tok, cols)), shape((sections, tok, width // sections))),
        in_specs=[smem] + [whole] * 4,
        out_specs=(whole,) * 2,
        compiler_params=vmem(),
        name="unpack",
    )(meta, image_offsets.reshape(1, frames), patch_counts.reshape(1, frames), keys_back, proj)

    summed = lax.all_to_all(terms, "phase", 0, 0, tiled=True)
    routed = pl.pallas_call(
        lambda *refs: route_kernel(frames, tok, *refs),
        out_shape=shape((frames, PATCH_MOST, HD)),
        in_specs=[smem, whole],
        out_specs=whole,
        scratch_shapes=[pltpu.VMEM((tok + PATCH_MOST, HD), F32)],
        compiler_params=vmem(),
        name="route",
    )(meta, summed)
    from_blocks = lax.all_to_all(routed, ("z", "y"), 0, 0, tiled=True)
    source = lax.dynamic_index_in_dim(image_offsets, block, keepdims=False) // tok
    d_slice = lax.dynamic_index_in_dim(from_blocks, source, keepdims=False)
    d_normed = lax.all_to_all(
        jnp.broadcast_to(d_slice[None], (sections,) + d_slice.shape), "phase", 0, 0, tiled=True
    )
    proj_rows = width // blocks
    proj_head = pl.pallas_call(
        proj_kernel,
        out_shape=shape((per, 2 * proj_rows, HD)),
        in_specs=[whole] * 2,
        out_specs=whole,
        compiler_params=vmem(),
        name="proj_grad",
    )(norm_pos, d_kv_all)
    proj_back = lax.all_to_all(proj_head, "y", 0, 0, tiled=True)
    d_proj = (
        proj_back[:heads].astype(F32)
        .reshape(heads, 2, proj_rows, HD)
        .transpose(2, 1, 0, 3)
        .reshape(proj_rows, 2, cols)
    )
    d_patches = pl.pallas_call(
        norm_grad_kernel,
        out_shape=shape(patches.shape),
        in_specs=[whole] * 3,
        out_specs=whole,
        compiler_params=vmem(),
        name="norm_grad",
    )(patches, gain, d_normed)
    return (
        att_here,
        dq_here,
        d_text_kv,
        d_proj,
        d_patches,
    )


def solution(mesh):
    sections, seq = mesh.devices.shape
    per = 4
    inner = Mesh(mesh.devices.reshape(sections, seq // per, per), ("phase", "z", "y"))
    seq = ("z", "y")
    return jax.shard_map(
        shards,
        mesh=inner,
        in_specs=(
            P(seq, None),
            P(),
            P(None, None, "phase"),
            P(seq, "phase"),
            P(None, seq, "phase"),
            P(None, "phase"),
            P(seq, "phase"),
            P(),
            P(),
            P(seq),
            P(),
        ),
        out_specs=(
            P(seq, "phase"),
            P(seq, "phase"),
            P(None, seq, "phase"),
            P(seq, None, "phase"),
            P(seq, None),
        ),
        check_vma=False,
    )
```

```python
import functools
import math

import jax
import jax.numpy as jnp
from jax import lax
from jax.experimental import pallas as pl
from jax.experimental.pallas import tpu as pltpu
from jax.sharding import Mesh
from jax.sharding import PartitionSpec as P

HD = 128
PAD = 256
PATCH_MOST = 64
EPISODES = 16
EPISODE_MOST = 2720
EPSILON = 1e-05
NEGATIVE = -1e30
CHUNK = 256
STAT_ROWS = 16

F32 = jnp.float32
BF16 = jnp.bfloat16


def dot_nt(a, b):
    return lax.dot_general(a, b, (((1,), (1,)), ((), ())), preferred_element_type=F32)


def dot_tn(a, b):
    return lax.dot_general(a, b, (((0,), (0,)), ((), ())), preferred_element_type=F32)


def dot_nn(a, b):
    return jnp.dot(a, b, preferred_element_type=F32)


def normalize_rows(patches):
    row_values = patches.astype(F32)
    center = row_values - jnp.mean(row_values, axis=-1, keepdims=True)
    inverse = lax.rsqrt(jnp.mean(center * center, axis=-1, keepdims=True) + EPSILON)
    return (center * inverse, inverse)


def vmem(limit=48):
    return pltpu.CompilerParams(vmem_limit_bytes=limit * 1024 * 1024)


def pack_kernel(heads, tok, patch_ref, gain_ref, proj_ref, q_ref, kv_ref, bias_ref, do_ref, type_ref,
                kv_out, q_out, normed_ref):
    scaled, _ = normalize_rows(patch_ref[0:PATCH_MOST])
    normed = (scaled * gain_ref[...]).astype(BF16)
    for i in range(normed_ref.shape[0]):
        normed_ref[i] = normed[:, i * HD : (i + 1) * HD]
    image = dot_nn(normed, proj_ref[...]).astype(BF16)
    cols = heads * HD
    bias = jnp.where(type_ref[...] == 1, bias_ref[1:2].astype(F32), bias_ref[0:1].astype(F32))
    keys = (kv_ref[0].astype(F32) + bias).astype(BF16)
    for h in range(heads):
        span = slice(h * HD, (h + 1) * HD)
        kv_out[h, 0:tok] = keys[:, span]
        kv_out[h, tok : 2 * tok] = kv_ref[1, :, span]
        kv_out[h, 2 * tok : 2 * tok + PATCH_MOST] = image[:, span]
        kv_out[h, 2 * tok + PATCH_MOST :] = image[:, cols + h * HD : cols + (h + 1) * HD]
        q_out[h, 0:tok] = q_ref[:, span]
        q_out[h, tok:] = do_ref[:, span]
    for h in range(heads, kv_out.shape[0]):
        kv_out[h] = jnp.zeros_like(kv_out[h])
        q_out[h] = jnp.zeros_like(q_out[h])


def place_kernel(frames, meta_ref, rows_ref, out_ref, scratch):
    total = out_ref.shape[1]
    per = rows_ref.shape[0]
    scratch[...] = jnp.zeros_like(scratch)
    row = lax.broadcasted_iota(jnp.int32, (PATCH_MOST, HD), 0)

    def one(f, carry):
        where = pl.ds(meta_ref[f], PATCH_MOST)
        live = row < meta_ref[frames + f]
        rows = rows_ref[lax.rem(f, per), lax.div(f, per)].astype(F32)
        scratch[where] = jnp.where(live, rows, scratch[where])
        return carry

    lax.fori_loop(0, frames, one, 0)

    def low(c, carry):
        where = pl.ds(pl.multiple_of(c * CHUNK, CHUNK), CHUNK)
        out_ref[:, where] = jnp.transpose(scratch[where]).astype(BF16)
        return carry

    lax.fori_loop(0, total // CHUNK, low, 0)


def query_kernel(frames, tok, meta_ref, start_ref, g_ref, mine_ref, out_hbm, own_hbm, stat_hbm,
                 out_ref, own_ref, stat_ref, out_sem, kf, vf, kb, vb, qb, dob, s_ref, m_ref, l_ref, acc):
    group = own_ref.shape[1]
    total = kb.shape[0]
    scale = 1.0 / math.sqrt(HD)
    power = scale * math.log2(math.e)
    z = meta_ref[2 * frames]
    first_chunk = meta_ref[2 * frames + 2]
    last_chunk = meta_ref[2 * frames + 3]
    image_row = 2 * tok

    def text(b, carry):
        where = pl.ds(pl.multiple_of(b * tok, 32), tok)
        kf[where] = g_ref[b, 0:tok].astype(F32)
        vf[where] = g_ref[b, tok : 2 * tok].astype(F32)
        return carry

    lax.fori_loop(0, total // tok, text, 0)
    row = lax.broadcasted_iota(jnp.int32, (PATCH_MOST, HD), 0)

    def image(f, carry):
        where = pl.ds(meta_ref[f], PATCH_MOST)
        live = row < meta_ref[frames + f]
        kf[where] = jnp.where(live, g_ref[f, image_row : image_row + PATCH_MOST].astype(F32), kf[where])
        vf[where] = jnp.where(live, g_ref[f, image_row + PATCH_MOST :].astype(F32), vf[where])
        return carry

    lax.fori_loop(0, frames, image, 0)

    def low(c, carry):
        where = pl.ds(pl.multiple_of(c * CHUNK, CHUNK), CHUNK)
        kb[where] = kf[where].astype(BF16)
        vb[where] = vf[where].astype(BF16)
        return carry

    lax.fori_loop(0, total // CHUNK, low, 0)
    per = group // tok
    for i in range(per):
        qb[i * tok : (i + 1) * tok] = mine_ref[i, 0:tok]
        dob[i * tok : (i + 1) * tok] = mine_ref[i, tok:]
    own = pl.ds(pl.multiple_of(z * group, HD), group)
    own_ref[0] = kb[own]
    own_ref[1] = vb[own]
    own_copy = pltpu.make_async_copy(own_ref, own_hbm, out_sem.at[0])
    own_copy.start()

    m_ref[...] = jnp.full_like(m_ref, NEGATIVE)
    l_ref[...] = jnp.zeros_like(l_ref)
    acc[...] = jnp.zeros_like(acc)
    lane = lax.broadcasted_iota(jnp.int32, (group, CHUNK), 1)
    query_pos = z * group + lax.broadcasted_iota(jnp.int32, (group, 1), 0)
    start = start_ref[...]

    def chunk(c):
        return pl.ds(pl.multiple_of(c * CHUNK, CHUNK), CHUNK)

    def scores(c, carry):
        s = dot_nt(qb[...], kb[chunk(c)])
        pos = lane + c * CHUNK
        s = jnp.where((pos >= start) & (pos <= query_pos), s, NEGATIVE)
        s_ref[c - first_chunk] = s
        m_ref[...] = jnp.maximum(m_ref[...], jnp.maximum(s[:, :HD], s[:, HD:]))
        return carry

    lax.fori_loop(first_chunk, last_chunk, scores, 0)
    row_max = jnp.max(m_ref[...], axis=1, keepdims=True)
    m_ref[...] = jnp.broadcast_to(row_max, m_ref.shape)

    def weigh(c, carry):
        top = m_ref[...]
        w = jnp.exp2((s_ref[c - first_chunk] - jnp.concatenate([top, top], axis=1)) * power)
        s_ref[c - first_chunk] = w
        l_ref[...] += w[:, :HD] + w[:, HD:]
        acc[...] += dot_nn(w.astype(BF16), vb[chunk(c)])
        return carry

    lax.fori_loop(first_chunk, last_chunk, weigh, 0)
    inverse_sum = 1.0 / jnp.sum(l_ref[...], axis=1, keepdims=True)
    attended = (acc[...] * inverse_sum).astype(BF16)
    for i in range(per):
        out_ref[i, 0:tok] = attended[i * tok : (i + 1) * tok]
    delta = jnp.sum(dob[...].astype(F32) * attended.astype(F32), axis=1, keepdims=True)
    acc[...] = jnp.zeros_like(acc)
    m_ref[...] = jnp.broadcast_to(inverse_sum, m_ref.shape)
    l_ref[...] = jnp.broadcast_to(delta, l_ref.shape)

    def back(c, carry):
        d_prob = dot_nt(dob[...], vb[chunk(c)])
        inv, dlt = m_ref[...], l_ref[...]
        p = s_ref[c - first_chunk] * jnp.concatenate([inv, inv], axis=1)
        d_score = (p * (d_prob - jnp.concatenate([dlt, dlt], axis=1))).astype(BF16)
        acc[...] += dot_nn(d_score, kb[chunk(c)])
        return carry

    lax.fori_loop(first_chunk, last_chunk, back, 0)
    d_query = (acc[...] * scale).astype(BF16)
    for i in range(per):
        out_ref[i, tok:] = d_query[i * tok : (i + 1) * tok]
    which = lax.broadcasted_iota(jnp.int32, (group, HD), 1)
    table = jnp.where(which == 0, row_max, jnp.where(which == 1, inverse_sum, delta))
    tiles = [jnp.transpose(table[i * HD : (i + 1) * HD])[0:8] for i in range(group // HD)]
    stat = jnp.concatenate([t[k : k + 1] for k in range(3) for t in tiles], axis=0)
    stat = jnp.concatenate([stat, stat[0:1]], axis=0)
    for i in range(stat_ref.shape[0]):
        stat_ref[i] = stat
    stat_copy = pltpu.make_async_copy(stat_ref, stat_hbm, out_sem.at[1])
    out_copy = pltpu.make_async_copy(out_ref, out_hbm, out_sem.at[2])
    stat_copy.start()
    out_copy.start()
    own_copy.wait()
    stat_copy.wait()
    out_copy.wait()


def key_kernel(frames, tok, meta_ref, end_ref, g_hbm, stat_hbm, own_hbm, dkv_hbm, out_hbm,
               qb, dob, stat_ref, own_ref, dk, dv, rows_ref, out_ref, q_sem, do_sem, in_sem, out_sem):
    group = own_ref.shape[1]
    per = group // tok
    scale = 1.0 / math.sqrt(HD)
    power = scale * math.log2(math.e)
    z = meta_ref[2 * frames]
    count = meta_ref[2 * frames + 5]
    last_tile = stat_ref.shape[0] * (group // HD) - 1

    def fetch(i):
        where = pl.ds(pl.multiple_of(i * tok, 32), tok)
        b = z * per + i
        return (
            pltpu.make_async_copy(g_hbm.at[b, 0:tok], qb.at[where], q_sem.at[i]),
            pltpu.make_async_copy(g_hbm.at[b, tok : 2 * tok], dob.at[where], do_sem.at[i]),
        )

    own_copy = pltpu.make_async_copy(own_hbm, own_ref, in_sem.at[0])
    stat_copy = pltpu.make_async_copy(stat_hbm, stat_ref, in_sem.at[1])
    own_copy.start()
    stat_copy.start()

    def begin(i, carry):
        for copy in fetch(i):
            copy.start()
        return carry

    def finish(i, carry):
        for copy in fetch(i):
            copy.wait()
        return carry

    lax.fori_loop(0, count, begin, 0)
    dk[...] = jnp.zeros_like(dk)
    dv[...] = jnp.zeros_like(dv)
    tail = pl.ds(pl.multiple_of(count * tok, 32), CHUNK)
    qb[tail] = jnp.zeros((CHUNK, HD), BF16)
    dob[tail] = jnp.zeros((CHUNK, HD), BF16)
    lane = lax.broadcasted_iota(jnp.int32, (group, CHUNK), 1)
    key_pos = lax.broadcasted_iota(jnp.int32, (group, 1), 0)
    end = end_ref[...] - z * group
    own_copy.wait()
    stat_copy.wait()

    def statistics(c, kind):
        parts = []
        for half in range(2):
            tile = jnp.minimum(z * (group // HD) + 2 * c + half, last_tile)
            at = lax.div(tile, group // HD)
            row = kind * (group // HD) + lax.rem(tile, group // HD)
            parts.append(stat_ref[at, pl.ds(row, 1)])
        return jnp.concatenate(parts, axis=1)

    def step(masked, c, carry):
        where = pl.ds(pl.multiple_of(c * CHUNK, CHUNK), CHUNK)
        arrived = lax.div(c * CHUNK + tok - 1, tok)
        needed = jnp.minimum(lax.div((c + 1) * CHUNK + tok - 1, tok), count)
        lax.fori_loop(arrived, needed, finish, 0)
        q, do = qb[where], dob[where]
        s = dot_nt(own_ref[0], q)
        p = jnp.exp2((s - statistics(c, 0)) * power) * statistics(c, 1)
        if masked:
            pos = lane + c * CHUNK
            p = jnp.where((pos >= key_pos) & (pos < end), p, 0.0)
        dv[...] += dot_nn(p.astype(BF16), do)
        d_prob = dot_nt(own_ref[1], do)
        d_score = (p * (d_prob - statistics(c, 2))).astype(BF16)
        dk[...] += dot_nn(d_score, q)
        return carry

    chunks = meta_ref[2 * frames + 4]
    after = jnp.minimum((group + CHUNK - 1) // CHUNK, chunks)
    shared = jnp.maximum(meta_ref[2 * frames + 6], after)
    lax.fori_loop(0, after, functools.partial(step, True), 0)
    lax.fori_loop(after, shared, functools.partial(step, False), 0)
    lax.fori_loop(shared, chunks, functools.partial(step, True), 0)
    key_grad = (dk[...] * scale).astype(BF16)
    value_grad = dv[...].astype(BF16)
    rows_ref[:, 0:HD] = key_grad
    rows_ref[:, HD:] = value_grad
    rows_copy = pltpu.make_async_copy(rows_ref, dkv_hbm, out_sem.at[0])
    rows_copy.start()
    for i in range(per):
        rows = slice(i * tok, (i + 1) * tok)
        out_ref[i, 0:tok] = key_grad[rows]
        out_ref[i, tok:] = value_grad[rows]
    out_copy = pltpu.make_async_copy(out_ref, out_hbm, out_sem.at[1])
    out_copy.start()
    rows_copy.wait()
    out_copy.wait()


def proj_kernel(norm_ref, grad_ref, out_ref):
    total = dot_nn(norm_ref[...], grad_ref[...])
    low = total.astype(BF16)
    rows = out_ref.shape[1] // 2
    for i in range(out_ref.shape[0]):
        out_ref[i, 0:rows] = low[i * rows : (i + 1) * rows, 0:HD]
        out_ref[i, rows:] = low[i * rows : (i + 1) * rows, HD:]


def unpack_queries_kernel(heads, tok, r_ref, att_ref, dq_ref):
    for h in range(heads):
        span = slice(h * HD, (h + 1) * HD)
        att_ref[:, span] = r_ref[h, 0:tok]
        dq_ref[:, span] = r_ref[h, tok:]


def unpack_kernel(heads, tok, meta_ref, offset_ref, count_ref, r_ref, proj_ref, dtext_ref, dn_ref):
    frames = offset_ref.shape[1]
    pos = meta_ref[2 * frames + 1] * tok + lax.broadcasted_iota(jnp.int32, (tok, frames), 0)
    begin = offset_ref[...]
    inside = (pos >= begin) & (pos < begin + count_ref[...])
    is_image = jnp.max(inside.astype(F32), axis=1, keepdims=True) > 0.5
    parts = [None] * (2 * heads)
    for h in range(heads):
        span = slice(h * HD, (h + 1) * HD)
        for c in range(2):
            grad = r_ref[h, c * tok : (c + 1) * tok]
            zero = jnp.zeros_like(grad)
            dtext_ref[c, :, span] = jnp.where(is_image, zero, grad)
            parts[c * heads + h] = jnp.where(is_image, grad, zero)
    grads = jnp.concatenate(parts, axis=1)
    for i in range(dn_ref.shape[0]):
        dn_ref[i] = dot_nt(grads, proj_ref[i * HD : (i + 1) * HD]).astype(BF16)


def sum_kernel(dn_ref, out_ref):
    total = dn_ref[0].astype(F32)
    for i in range(1, dn_ref.shape[0]):
        total = total + dn_ref[i].astype(F32)
    low = total.astype(BF16)
    for i in range(out_ref.shape[0]):
        out_ref[i] = low


def route_kernel(frames, meta_ref, rows_ref, out_ref, scratch):
    per, tok = rows_ref.shape[0], rows_ref.shape[1]
    group = per * tok
    z = meta_ref[2 * frames]
    y = meta_ref[2 * frames + 1] - z * per
    for i in range(per):
        scratch[i * tok : (i + 1) * tok] = rows_ref[i].astype(F32)
    scratch[group:] = jnp.zeros((PATCH_MOST, HD), F32)
    row = lax.broadcasted_iota(jnp.int32, (PATCH_MOST, HD), 0)
    for i in range(out_ref.shape[0]):
        f = i * per + y
        offset = meta_ref[f] - z * group
        here = (offset >= 0) & (offset < group)
        live = jnp.where(here, meta_ref[frames + f], 0)
        rows = scratch[pl.ds(jnp.where(here, offset, 0), PATCH_MOST)]
        out_ref[i] = jnp.where(row < live, rows, 0.0).astype(BF16)


def norm_grad_kernel(patch_ref, gain_ref, dn_ref, out_ref):
    scaled, inverse = normalize_rows(patch_ref[0:PATCH_MOST])
    d_normed = jnp.concatenate([dn_ref[i] for i in range(dn_ref.shape[0])], axis=1).astype(F32)
    scaled_grad = d_normed * gain_ref[...]
    d_rows = (
        scaled_grad
        - jnp.mean(scaled_grad, axis=-1, keepdims=True)
        - scaled * jnp.mean(scaled_grad * scaled, axis=-1, keepdims=True)
    ) * inverse
    out_ref[0:PATCH_MOST] = d_rows.astype(BF16)
    out_ref[PATCH_MOST:] = jnp.zeros((out_ref.shape[0] - PATCH_MOST, out_ref.shape[1]), BF16)


def shards(patches, ln_gain, kv_proj, query, text_kv, type_bias, d_out, patch_counts, image_offsets,
           token_types, segment_ids):
    tok, cols = query.shape
    heads = cols // HD
    width = patches.shape[1]
    groups, per, sections = lax.axis_size("z"), lax.axis_size("y"), lax.axis_size("phase")
    frames = patch_counts.shape[0]
    blocks = groups * per
    group = per * tok
    total = blocks * tok
    z, y, section = lax.axis_index("z"), lax.axis_index("y"), lax.axis_index("phase")
    block = z * per + y
    smem = pl.BlockSpec(memory_space=pltpu.SMEM)
    whole = pl.BlockSpec(memory_space=pltpu.VMEM)
    hbm = pl.BlockSpec(memory_space=pltpu.HBM)

    def shape(dims, kind=BF16):
        return jax.ShapeDtypeStruct(dims, kind)

    ids = jnp.arange(EPISODES, dtype=jnp.int32)
    seg_first = jnp.sum((segment_ids[None, :] < ids[:, None]).astype(jnp.int32), axis=1)
    seg_end = jnp.sum((segment_ids[None, :] <= ids[:, None]).astype(jnp.int32), axis=1)
    own_seg = lax.dynamic_slice_in_dim(segment_ids, z * group, group)
    same = own_seg[:, None] == ids[None, :]
    start = jnp.sum(jnp.where(same, seg_first[None, :], 0), axis=1, keepdims=True)
    end = jnp.sum(jnp.where(same, seg_end[None, :], 0), axis=1, keepdims=True)
    scalars = jnp.stack([
        z,
        block,
        start[0, 0] // CHUNK,
        ((z + 1) * group + CHUNK - 1) // CHUNK,
        (end[group - 1, 0] - z * group + CHUNK - 1) // CHUNK,
        (end[group - 1, 0] - z * group + tok - 1) // tok,
        (end[0, 0] - z * group) // CHUNK,
    ]).astype(jnp.int32)
    meta = jnp.concatenate([image_offsets, patch_counts, scalars])
    gain = ln_gain.reshape(1, width)
    proj = kv_proj.reshape(width, 2 * cols)
    packed, questions, normed = pl.pallas_call(
        lambda *refs: pack_kernel(heads, tok, *refs),
        out_shape=(
            shape((per, 2 * tok + 2 * PATCH_MOST, HD)),
            shape((per, 2 * tok, HD)),
            shape((groups, PATCH_MOST, HD)),
        ),
        in_specs=[whole] * 8,
        out_specs=(whole, whole, whole),
        compiler_params=vmem(),
        name="pack",
    )(patches, gain, proj, query, text_kv, type_bias, d_out, token_types.reshape(tok, 1))
    kv_mine = lax.all_to_all(packed, "y", 0, 0, tiled=True)
    kv_all = lax.all_gather(kv_mine, "z", axis=0, tiled=True)
    questions, _ = lax.optimization_barrier((questions, kv_mine))
    q_mine = lax.all_to_all(questions, "y", 0, 0, tiled=True)
    q_all = lax.all_gather(q_mine, "z", axis=0, tiled=True)

    normed, _ = lax.optimization_barrier((normed, q_mine))
    some_frames = lax.all_to_all(normed, "z", 0, 0, tiled=True)
    all_frames = lax.all_gather(some_frames, "y", axis=0, tiled=False)
    norm_pos = pl.pallas_call(
        lambda *refs: place_kernel(frames, *refs),
        out_shape=shape((HD, total)),
        in_specs=[smem, whole],
        out_specs=whole,
        scratch_shapes=[pltpu.VMEM((total + PATCH_MOST, HD), F32)],
        compiler_params=vmem(),
        name="place",
    )(meta, all_frames)
    kv_all, norm_pos = lax.optimization_barrier((kv_all, norm_pos))

    most_blocks = (group - 1 + EPISODE_MOST + tok - 1) // tok
    most_chunks = (EPISODE_MOST + group + CHUNK - 2) // CHUNK + 1
    answers, own_kv, stats = pl.pallas_call(
        lambda *refs: query_kernel(frames, tok, *refs),
        out_shape=(
            shape((per, 2 * tok, HD)),
            shape((2, group, HD)),
            shape((groups, STAT_ROWS, HD), F32),
        ),
        in_specs=[smem, whole, whole, whole],
        out_specs=(hbm, hbm, hbm),
        scratch_shapes=[
            pltpu.VMEM((per, 2 * tok, HD), BF16),
            pltpu.VMEM((2, group, HD), BF16),
            pltpu.VMEM((groups, STAT_ROWS, HD), F32),
            pltpu.SemaphoreType.DMA((3,)),
            pltpu.VMEM((total + PATCH_MOST, HD), F32),
            pltpu.VMEM((total + PATCH_MOST, HD), F32),
            pltpu.VMEM((total, HD), BF16),
            pltpu.VMEM((total, HD), BF16),
            pltpu.VMEM((group, HD), BF16),
            pltpu.VMEM((group, HD), BF16),
            pltpu.VMEM((most_chunks, group, CHUNK), F32),
            pltpu.VMEM((group, HD), F32),
            pltpu.VMEM((group, HD), F32),
            pltpu.VMEM((group, HD), F32),
        ],
        compiler_params=vmem(62),
        name="queries",
    )(meta, start, kv_all, q_mine)
    all_stats = lax.all_to_all(stats, "z", 0, 0, tiled=True)
    answers, all_stats = lax.optimization_barrier((answers, all_stats))
    returned = lax.all_to_all(answers, "y", 0, 0, tiled=True)
    att_here, dq_here = pl.pallas_call(
        lambda *refs: unpack_queries_kernel(heads, tok, *refs),
        out_shape=(shape((tok, cols)), shape((tok, cols))),
        in_specs=[whole],
        out_specs=(whole, whole),
        compiler_params=vmem(),
        name="unpack_queries",
    )(returned)
    q_all, returned = lax.optimization_barrier((q_all, returned))

    d_kv, key_grads = pl.pallas_call(
        lambda *refs: key_kernel(frames, tok, *refs),
        out_shape=(shape((group, 2 * HD)), shape((per, 2 * tok, HD))),
        in_specs=[smem, whole, hbm, hbm, hbm],
        out_specs=(hbm, hbm),
        scratch_shapes=[
            pltpu.VMEM((most_blocks * tok + CHUNK, HD), BF16),
            pltpu.VMEM((most_blocks * tok + CHUNK, HD), BF16),
            pltpu.VMEM((groups, STAT_ROWS, HD), F32),
            pltpu.VMEM((2, group, HD), BF16),
            pltpu.VMEM((group, HD), F32),
            pltpu.VMEM((group, HD), F32),
            pltpu.VMEM((group, 2 * HD), BF16),
            pltpu.VMEM((per, 2 * tok, HD), BF16),
            pltpu.SemaphoreType.DMA((most_blocks,)),
            pltpu.SemaphoreType.DMA((most_blocks,)),
            pltpu.SemaphoreType.DMA((2,)),
            pltpu.SemaphoreType.DMA((2,)),
        ],
        compiler_params=vmem(62),
        name="keys",
    )(meta, end, q_all, all_stats, own_kv)
    d_kv_all = lax.all_gather(d_kv, "z", axis=0, tiled=True)
    keys_back = lax.all_to_all(key_grads, "y", 0, 0, tiled=True)
    d_text_kv, terms = pl.pallas_call(
        lambda *refs: unpack_kernel(heads, tok, *refs),
        out_shape=(shape((2, tok, cols)), shape((sections, tok, width // sections))),
        in_specs=[smem] + [whole] * 4,
        out_specs=(whole,) * 2,
        compiler_params=vmem(),
        name="unpack",
    )(meta, image_offsets.reshape(1, frames), patch_counts.reshape(1, frames), keys_back, proj)

    summed = lax.all_to_all(terms, "phase", 0, 0, tiled=True)
    here = pl.pallas_call(
        sum_kernel,
        out_shape=shape((per, tok, HD)),
        in_specs=[whole],
        out_specs=whole,
        compiler_params=vmem(),
        name="sum",
    )(summed)
    of_group = lax.all_to_all(here, "y", 0, 0, tiled=True)
    routed = pl.pallas_call(
        lambda *refs: route_kernel(frames, *refs),
        out_shape=shape((groups, PATCH_MOST, HD)),
        in_specs=[smem, whole],
        out_specs=whole,
        scratch_shapes=[pltpu.VMEM((group + PATCH_MOST, HD), F32)],
        compiler_params=vmem(),
        name="route",
    )(meta, of_group)
    from_groups = lax.all_to_all(routed, "z", 0, 0, tiled=True)
    source = lax.dynamic_index_in_dim(image_offsets, block, keepdims=False) // group
    d_slice = lax.dynamic_index_in_dim(from_groups, source, keepdims=False)
    d_normed = lax.all_to_all(
        jnp.broadcast_to(d_slice[None], (sections,) + d_slice.shape), "phase", 0, 0, tiled=True
    )
    proj_rows = width // blocks
    proj_head = pl.pallas_call(
        proj_kernel,
        out_shape=shape((per, 2 * proj_rows, HD)),
        in_specs=[whole, whole],
        out_specs=whole,
        compiler_params=vmem(),
        name="proj_grad",
    )(norm_pos, d_kv_all)
    proj_back = lax.all_to_all(proj_head, "y", 0, 0, tiled=True)
    d_proj = (
        proj_back[:heads].astype(F32)
        .reshape(heads, 2, proj_rows, HD)
        .transpose(2, 1, 0, 3)
        .reshape(proj_rows, 2, cols)
    )
    d_patches = pl.pallas_call(
        norm_grad_kernel,
        out_shape=shape(patches.shape),
        in_specs=[whole] * 3,
        out_specs=whole,
        compiler_params=vmem(),
        name="norm_grad",
    )(patches, gain, d_normed)
    return (
        att_here,
        dq_here,
        d_text_kv,
        d_proj,
        d_patches,
    )


def solution(mesh):
    sections, seq = mesh.devices.shape
    per = 4
    inner = Mesh(mesh.devices.reshape(sections, seq // per, per), ("phase", "z", "y"))
    seq = ("z", "y")
    return jax.shard_map(
        shards,
        mesh=inner,
        in_specs=(
            P(seq, None),
            P(),
            P(None, None, "phase"),
            P(seq, "phase"),
            P(None, seq, "phase"),
            P(None, "phase"),
            P(seq, "phase"),
            P(),
            P(),
            P(seq),
            P(),
        ),
        out_specs=(
            P(seq, "phase"),
            P(seq, "phase"),
            P(None, seq, "phase"),
            P(seq, None, "phase"),
            P(seq, None),
        ),
        check_vma=False,
    )
```

```python
import functools
import math

import jax
import jax.numpy as jnp
from jax import lax
from jax.experimental import pallas as pl
from jax.experimental.pallas import tpu as pltpu
from jax.sharding import Mesh
from jax.sharding import PartitionSpec as P

HD = 128
PAD = 256
PATCH_MOST = 64
EPISODES = 16
EPISODE_MOST = 2720
EPSILON = 1e-05
NEGATIVE = -1e30
CHUNK = 256
KEY_CHUNK = 512
STAT_ROWS = 16

F32 = jnp.float32
BF16 = jnp.bfloat16


def dot_nt(a, b):
    return lax.dot_general(a, b, (((1,), (1,)), ((), ())), preferred_element_type=F32)


def dot_tn(a, b):
    return lax.dot_general(a, b, (((0,), (0,)), ((), ())), preferred_element_type=F32)


def dot_nn(a, b):
    return jnp.dot(a, b, preferred_element_type=F32)


def normalize_rows(patches):
    row_values = patches.astype(F32)
    center = row_values - jnp.mean(row_values, axis=-1, keepdims=True)
    inverse = lax.rsqrt(jnp.mean(center * center, axis=-1, keepdims=True) + EPSILON)
    return (center * inverse, inverse)


def vmem(limit=48):
    return pltpu.CompilerParams(vmem_limit_bytes=limit * 1024 * 1024)


def pack_kernel(heads, tok, patch_ref, gain_ref, proj_ref, q_ref, kv_ref, bias_ref, do_ref, type_ref,
                kv_out, q_out, normed_ref):
    scaled, _ = normalize_rows(patch_ref[0:PATCH_MOST])
    normed = (scaled * gain_ref[...]).astype(BF16)
    for i in range(normed_ref.shape[0]):
        normed_ref[i] = normed[:, i * HD : (i + 1) * HD]
    image = dot_nn(normed, proj_ref[...]).astype(BF16)
    cols = heads * HD
    bias = jnp.where(type_ref[...] == 1, bias_ref[1:2].astype(F32), bias_ref[0:1].astype(F32))
    keys = (kv_ref[0].astype(F32) + bias).astype(BF16)
    for h in range(heads):
        span = slice(h * HD, (h + 1) * HD)
        kv_out[h, 0:tok] = keys[:, span]
        kv_out[h, tok : 2 * tok] = kv_ref[1, :, span]
        kv_out[h, 2 * tok : 2 * tok + PATCH_MOST] = image[:, span]
        kv_out[h, 2 * tok + PATCH_MOST :] = image[:, cols + h * HD : cols + (h + 1) * HD]
        q_out[h, 0:tok] = q_ref[:, span]
        q_out[h, tok:] = do_ref[:, span]
    for h in range(heads, kv_out.shape[0]):
        kv_out[h] = jnp.zeros_like(kv_out[h])
        q_out[h] = jnp.zeros_like(q_out[h])


def place_kernel(frames, meta_ref, rows_ref, out_ref, scratch):
    total = out_ref.shape[1]
    per = rows_ref.shape[0]
    scratch[...] = jnp.zeros_like(scratch)
    row = lax.broadcasted_iota(jnp.int32, (PATCH_MOST, HD), 0)

    def one(f, carry):
        where = pl.ds(meta_ref[f], PATCH_MOST)
        live = row < meta_ref[frames + f]
        rows = rows_ref[lax.rem(f, per), lax.div(f, per)].astype(F32)
        scratch[where] = jnp.where(live, rows, scratch[where])
        return carry

    lax.fori_loop(0, frames, one, 0)

    def low(c, carry):
        where = pl.ds(pl.multiple_of(c * CHUNK, CHUNK), CHUNK)
        out_ref[:, where] = jnp.transpose(scratch[where]).astype(BF16)
        return carry

    lax.fori_loop(0, total // CHUNK, low, 0)


def query_kernel(frames, tok, meta_ref, start_ref, g_ref, mine_ref, out_hbm, own_hbm, stat_hbm,
                 out_ref, own_ref, stat_ref, out_sem, kf, vf, kb, vb, qb, dob, s_ref, m_ref, l_ref, acc):
    group = own_ref.shape[1]
    total = kb.shape[0]
    scale = 1.0 / math.sqrt(HD)
    power = scale * math.log2(math.e)
    z = meta_ref[2 * frames]
    first_chunk = meta_ref[2 * frames + 2]
    last_chunk = meta_ref[2 * frames + 3]
    image_row = 2 * tok

    def text(b, carry):
        where = pl.ds(pl.multiple_of(b * tok, 32), tok)
        kf[where] = g_ref[b, 0:tok].astype(F32)
        vf[where] = g_ref[b, tok : 2 * tok].astype(F32)
        return carry

    lax.fori_loop(0, total // tok, text, 0)
    row = lax.broadcasted_iota(jnp.int32, (PATCH_MOST, HD), 0)

    def image(f, carry):
        where = pl.ds(meta_ref[f], PATCH_MOST)
        live = row < meta_ref[frames + f]
        kf[where] = jnp.where(live, g_ref[f, image_row : image_row + PATCH_MOST].astype(F32), kf[where])
        vf[where] = jnp.where(live, g_ref[f, image_row + PATCH_MOST :].astype(F32), vf[where])
        return carry

    lax.fori_loop(0, frames, image, 0)

    def low(c, carry):
        where = pl.ds(pl.multiple_of(c * CHUNK, CHUNK), CHUNK)
        kb[where] = kf[where].astype(BF16)
        vb[where] = vf[where].astype(BF16)
        return carry

    lax.fori_loop(0, total // CHUNK, low, 0)
    per = group // tok
    for i in range(per):
        qb[i * tok : (i + 1) * tok] = mine_ref[i, 0:tok]
        dob[i * tok : (i + 1) * tok] = mine_ref[i, tok:]
    own = pl.ds(pl.multiple_of(z * group, HD), group)
    own_ref[0] = kb[own]
    own_ref[1] = vb[own]
    own_copy = pltpu.make_async_copy(own_ref, own_hbm, out_sem.at[0])
    own_copy.start()

    m_ref[...] = jnp.full_like(m_ref, NEGATIVE)
    l_ref[...] = jnp.zeros_like(l_ref)
    acc[...] = jnp.zeros_like(acc)
    lane = lax.broadcasted_iota(jnp.int32, (group, CHUNK), 1)
    query_pos = z * group + lax.broadcasted_iota(jnp.int32, (group, 1), 0)
    start = start_ref[...]

    def chunk(c):
        return pl.ds(pl.multiple_of(c * CHUNK, CHUNK), CHUNK)

    def scores(c, carry):
        s = dot_nt(qb[...], kb[chunk(c)])
        pos = lane + c * CHUNK
        s = jnp.where((pos >= start) & (pos <= query_pos), s, NEGATIVE)
        s_ref[c - first_chunk] = s
        m_ref[...] = jnp.maximum(m_ref[...], jnp.maximum(s[:, :HD], s[:, HD:]))
        return carry

    lax.fori_loop(first_chunk, last_chunk, scores, 0)
    row_max = jnp.max(m_ref[...], axis=1, keepdims=True)
    m_ref[...] = jnp.broadcast_to(row_max, m_ref.shape)

    def weigh(c, carry):
        top = m_ref[...]
        w = jnp.exp2((s_ref[c - first_chunk] - jnp.concatenate([top, top], axis=1)) * power)
        s_ref[c - first_chunk] = w
        l_ref[...] += w[:, :HD] + w[:, HD:]
        acc[...] += dot_nn(w.astype(BF16), vb[chunk(c)])
        return carry

    lax.fori_loop(first_chunk, last_chunk, weigh, 0)
    inverse_sum = 1.0 / jnp.sum(l_ref[...], axis=1, keepdims=True)
    attended = (acc[...] * inverse_sum).astype(BF16)
    for i in range(per):
        out_ref[i, 0:tok] = attended[i * tok : (i + 1) * tok]
    delta = jnp.sum(dob[...].astype(F32) * attended.astype(F32), axis=1, keepdims=True)
    acc[...] = jnp.zeros_like(acc)
    m_ref[...] = jnp.broadcast_to(inverse_sum, m_ref.shape)
    l_ref[...] = jnp.broadcast_to(delta, l_ref.shape)

    def back(c, carry):
        d_prob = dot_nt(dob[...], vb[chunk(c)])
        inv, dlt = m_ref[...], l_ref[...]
        p = s_ref[c - first_chunk] * jnp.concatenate([inv, inv], axis=1)
        d_score = (p * (d_prob - jnp.concatenate([dlt, dlt], axis=1))).astype(BF16)
        acc[...] += dot_nn(d_score, kb[chunk(c)])
        return carry

    lax.fori_loop(first_chunk, last_chunk, back, 0)
    d_query = (acc[...] * scale).astype(BF16)
    for i in range(per):
        out_ref[i, tok:] = d_query[i * tok : (i + 1) * tok]
    which = lax.broadcasted_iota(jnp.int32, (group, HD), 1)
    table = jnp.where(which == 0, row_max, jnp.where(which == 1, inverse_sum, delta))
    tiles = [jnp.transpose(table[i * HD : (i + 1) * HD])[0:8] for i in range(group // HD)]
    stat = jnp.concatenate([t[k : k + 1] for k in range(3) for t in tiles], axis=0)
    stat = jnp.concatenate([stat, stat[0:1]], axis=0)
    for i in range(stat_ref.shape[0]):
        stat_ref[i] = stat
    stat_copy = pltpu.make_async_copy(stat_ref, stat_hbm, out_sem.at[1])
    out_copy = pltpu.make_async_copy(out_ref, out_hbm, out_sem.at[2])
    stat_copy.start()
    out_copy.start()
    own_copy.wait()
    stat_copy.wait()
    out_copy.wait()


def key_kernel(frames, tok, meta_ref, end_ref, g_hbm, stat_hbm, own_hbm, dkv_hbm, out_hbm,
               qb, dob, stat_ref, own_ref, dk, dv, rows_ref, out_ref, q_sem, do_sem, in_sem, out_sem):
    group = own_ref.shape[1]
    per = group // tok
    scale = 1.0 / math.sqrt(HD)
    power = scale * math.log2(math.e)
    z = meta_ref[2 * frames]
    count = meta_ref[2 * frames + 5]
    last_tile = stat_ref.shape[0] * (group // HD) - 1

    def fetch(i):
        where = pl.ds(pl.multiple_of(i * tok, 32), tok)
        b = z * per + i
        return (
            pltpu.make_async_copy(g_hbm.at[b, 0:tok], qb.at[where], q_sem.at[i]),
            pltpu.make_async_copy(g_hbm.at[b, tok : 2 * tok], dob.at[where], do_sem.at[i]),
        )

    own_copy = pltpu.make_async_copy(own_hbm, own_ref, in_sem.at[0])
    stat_copy = pltpu.make_async_copy(stat_hbm, stat_ref, in_sem.at[1])
    own_copy.start()
    stat_copy.start()

    def begin(i, carry):
        for copy in fetch(i):
            copy.start()
        return carry

    def finish(i, carry):
        for copy in fetch(i):
            copy.wait()
        return carry

    lax.fori_loop(0, count, begin, 0)
    dk[...] = jnp.zeros_like(dk)
    dv[...] = jnp.zeros_like(dv)
    tail = pl.ds(pl.multiple_of(count * tok, 32), KEY_CHUNK)
    qb[tail] = jnp.zeros((KEY_CHUNK, HD), BF16)
    dob[tail] = jnp.zeros((KEY_CHUNK, HD), BF16)
    lane = lax.broadcasted_iota(jnp.int32, (group, KEY_CHUNK), 1)
    key_pos = lax.broadcasted_iota(jnp.int32, (group, 1), 0)
    end = end_ref[...] - z * group
    own_copy.wait()
    stat_copy.wait()

    def statistics(c, kind):
        parts = []
        for half in range(KEY_CHUNK // HD):
            tile = jnp.minimum(z * (group // HD) + (KEY_CHUNK // HD) * c + half, last_tile)
            at = lax.div(tile, group // HD)
            row = kind * (group // HD) + lax.rem(tile, group // HD)
            parts.append(stat_ref[at, pl.ds(row, 1)])
        return jnp.concatenate(parts, axis=1)

    def step(masked, c, carry):
        where = pl.ds(pl.multiple_of(c * KEY_CHUNK, KEY_CHUNK), KEY_CHUNK)
        arrived = lax.div(c * KEY_CHUNK + tok - 1, tok)
        needed = jnp.minimum(lax.div((c + 1) * KEY_CHUNK + tok - 1, tok), count)
        lax.fori_loop(arrived, needed, finish, 0)
        q, do = qb[where], dob[where]
        s = dot_nt(own_ref[0], q)
        p = jnp.exp2((s - statistics(c, 0)) * power) * statistics(c, 1)
        if masked:
            pos = lane + c * KEY_CHUNK
            p = jnp.where((pos >= key_pos) & (pos < end), p, 0.0)
        dv[...] += dot_nn(p.astype(BF16), do)
        d_prob = dot_nt(own_ref[1], do)
        d_score = (p * (d_prob - statistics(c, 2))).astype(BF16)
        dk[...] += dot_nn(d_score, q)
        return carry

    chunks = meta_ref[2 * frames + 4]
    after = jnp.minimum((group + KEY_CHUNK - 1) // KEY_CHUNK, chunks)
    shared = jnp.maximum(meta_ref[2 * frames + 6], after)
    lax.fori_loop(0, after, functools.partial(step, True), 0)
    lax.fori_loop(after, shared, functools.partial(step, False), 0)
    lax.fori_loop(shared, chunks, functools.partial(step, True), 0)
    key_grad = (dk[...] * scale).astype(BF16)
    value_grad = dv[...].astype(BF16)
    rows_ref[:, 0:HD] = key_grad
    rows_ref[:, HD:] = value_grad
    rows_copy = pltpu.make_async_copy(rows_ref, dkv_hbm, out_sem.at[0])
    rows_copy.start()
    for i in range(per):
        rows = slice(i * tok, (i + 1) * tok)
        out_ref[i, 0:tok] = key_grad[rows]
        out_ref[i, tok:] = value_grad[rows]
    out_copy = pltpu.make_async_copy(out_ref, out_hbm, out_sem.at[1])
    out_copy.start()
    rows_copy.wait()
    out_copy.wait()


def proj_kernel(norm_ref, grad_ref, out_ref):
    total = dot_nn(norm_ref[...], grad_ref[...])
    low = total.astype(BF16)
    rows = out_ref.shape[1] // 2
    for i in range(out_ref.shape[0]):
        out_ref[i, 0:rows] = low[i * rows : (i + 1) * rows, 0:HD]
        out_ref[i, rows:] = low[i * rows : (i + 1) * rows, HD:]


def unpack_queries_kernel(heads, tok, r_ref, att_ref, dq_ref):
    for h in range(heads):
        span = slice(h * HD, (h + 1) * HD)
        att_ref[:, span] = r_ref[h, 0:tok]
        dq_ref[:, span] = r_ref[h, tok:]


def unpack_kernel(heads, tok, meta_ref, offset_ref, count_ref, r_ref, proj_ref, dtext_ref, dn_ref):
    frames = offset_ref.shape[1]
    pos = meta_ref[2 * frames + 1] * tok + lax.broadcasted_iota(jnp.int32, (tok, frames), 0)
    begin = offset_ref[...]
    inside = (pos >= begin) & (pos < begin + count_ref[...])
    is_image = jnp.max(inside.astype(F32), axis=1, keepdims=True) > 0.5
    parts = [None] * (2 * heads)
    for h in range(heads):
        span = slice(h * HD, (h + 1) * HD)
        for c in range(2):
            grad = r_ref[h, c * tok : (c + 1) * tok]
            zero = jnp.zeros_like(grad)
            dtext_ref[c, :, span] = jnp.where(is_image, zero, grad)
            parts[c * heads + h] = jnp.where(is_image, grad, zero)
    grads = jnp.concatenate(parts, axis=1)
    for i in range(dn_ref.shape[0]):
        dn_ref[i] = dot_nt(grads, proj_ref[i * HD : (i + 1) * HD]).astype(BF16)


def sum_kernel(dn_ref, out_ref):
    total = dn_ref[0].astype(F32)
    for i in range(1, dn_ref.shape[0]):
        total = total + dn_ref[i].astype(F32)
    low = total.astype(BF16)
    for i in range(out_ref.shape[0]):
        out_ref[i] = low


def route_kernel(frames, meta_ref, rows_ref, out_ref, scratch):
    per, tok = rows_ref.shape[0], rows_ref.shape[1]
    group = per * tok
    z = meta_ref[2 * frames]
    y = meta_ref[2 * frames + 1] - z * per
    for i in range(per):
        scratch[i * tok : (i + 1) * tok] = rows_ref[i].astype(F32)
    scratch[group:] = jnp.zeros((PATCH_MOST, HD), F32)
    row = lax.broadcasted_iota(jnp.int32, (PATCH_MOST, HD), 0)
    for i in range(out_ref.shape[0]):
        f = i * per + y
        offset = meta_ref[f] - z * group
        here = (offset >= 0) & (offset < group)
        live = jnp.where(here, meta_ref[frames + f], 0)
        rows = scratch[pl.ds(jnp.where(here, offset, 0), PATCH_MOST)]
        out_ref[i] = jnp.where(row < live, rows, 0.0).astype(BF16)


def pick_kernel(frames, group, meta_ref, rows_ref, out_ref):
    rows = rows_ref[lax.div(meta_ref[meta_ref[2 * frames + 1]], group)]
    for i in range(out_ref.shape[0]):
        out_ref[i] = rows


def proj_out_kernel(heads, r_ref, out_ref):
    rows = out_ref.shape[0]
    for h in range(heads):
        for c in range(2):
            part = r_ref[h, c * rows : (c + 1) * rows].astype(F32)
            out_ref[:, c, h * HD : (h + 1) * HD] = part


def norm_grad_kernel(patch_ref, gain_ref, dn_ref, out_ref):
    scaled, inverse = normalize_rows(patch_ref[0:PATCH_MOST])
    d_normed = jnp.concatenate([dn_ref[i] for i in range(dn_ref.shape[0])], axis=1).astype(F32)
    scaled_grad = d_normed * gain_ref[...]
    d_rows = (
        scaled_grad
        - jnp.mean(scaled_grad, axis=-1, keepdims=True)
        - scaled * jnp.mean(scaled_grad * scaled, axis=-1, keepdims=True)
    ) * inverse
    out_ref[0:PATCH_MOST] = d_rows.astype(BF16)
    out_ref[PATCH_MOST:] = jnp.zeros((out_ref.shape[0] - PATCH_MOST, out_ref.shape[1]), BF16)


def shards(patches, ln_gain, kv_proj, query, text_kv, type_bias, d_out, patch_counts, image_offsets,
           token_types, segment_ids):
    tok, cols = query.shape
    heads = cols // HD
    width = patches.shape[1]
    groups, per, sections = lax.axis_size("z"), lax.axis_size("y"), lax.axis_size("phase")
    frames = patch_counts.shape[0]
    blocks = groups * per
    group = per * tok
    total = blocks * tok
    z, y, section = lax.axis_index("z"), lax.axis_index("y"), lax.axis_index("phase")
    block = z * per + y
    smem = pl.BlockSpec(memory_space=pltpu.SMEM)
    whole = pl.BlockSpec(memory_space=pltpu.VMEM)
    hbm = pl.BlockSpec(memory_space=pltpu.HBM)

    def shape(dims, kind=BF16):
        return jax.ShapeDtypeStruct(dims, kind)

    ids = jnp.arange(EPISODES, dtype=jnp.int32)
    seg_first = jnp.sum((segment_ids[None, :] < ids[:, None]).astype(jnp.int32), axis=1)
    seg_end = jnp.sum((segment_ids[None, :] <= ids[:, None]).astype(jnp.int32), axis=1)
    own_seg = lax.dynamic_slice_in_dim(segment_ids, z * group, group)
    same = own_seg[:, None] == ids[None, :]
    start = jnp.sum(jnp.where(same, seg_first[None, :], 0), axis=1, keepdims=True)
    end = jnp.sum(jnp.where(same, seg_end[None, :], 0), axis=1, keepdims=True)
    scalars = jnp.stack([
        z,
        block,
        start[0, 0] // CHUNK,
        ((z + 1) * group + CHUNK - 1) // CHUNK,
        (end[group - 1, 0] - z * group + KEY_CHUNK - 1) // KEY_CHUNK,
        (end[group - 1, 0] - z * group + tok - 1) // tok,
        (end[0, 0] - z * group) // KEY_CHUNK,
    ]).astype(jnp.int32)
    meta = jnp.concatenate([image_offsets, patch_counts, scalars])
    gain = ln_gain.reshape(1, width)
    proj = kv_proj.reshape(width, 2 * cols)
    packed, questions, normed = pl.pallas_call(
        lambda *refs: pack_kernel(heads, tok, *refs),
        out_shape=(
            shape((per, 2 * tok + 2 * PATCH_MOST, HD)),
            shape((per, 2 * tok, HD)),
            shape((groups, PATCH_MOST, HD)),
        ),
        in_specs=[whole] * 8,
        out_specs=(whole, whole, whole),
        compiler_params=vmem(),
        name="pack",
    )(patches, gain, proj, query, text_kv, type_bias, d_out, token_types.reshape(tok, 1))
    kv_mine = lax.all_to_all(packed, "y", 0, 0, tiled=True)
    kv_all = lax.all_gather(kv_mine, "z", axis=0, tiled=True)
    questions, _ = lax.optimization_barrier((questions, kv_mine))
    q_mine = lax.all_to_all(questions, "y", 0, 0, tiled=True)
    q_all = lax.all_gather(q_mine, "z", axis=0, tiled=True)

    normed, _ = lax.optimization_barrier((normed, q_mine))
    some_frames = lax.all_to_all(normed, "z", 0, 0, tiled=True)
    all_frames = lax.all_gather(some_frames, "y", axis=0, tiled=False)
    norm_pos = pl.pallas_call(
        lambda *refs: place_kernel(frames, *refs),
        out_shape=shape((HD, total)),
        in_specs=[smem, whole],
        out_specs=whole,
        scratch_shapes=[pltpu.VMEM((total + PATCH_MOST, HD), F32)],
        compiler_params=vmem(),
        name="place",
    )(meta, all_frames)
    kv_all, norm_pos = lax.optimization_barrier((kv_all, norm_pos))

    most_blocks = (group - 1 + EPISODE_MOST + tok - 1) // tok
    most_chunks = (EPISODE_MOST + group + CHUNK - 2) // CHUNK + 1
    answers, own_kv, stats = pl.pallas_call(
        lambda *refs: query_kernel(frames, tok, *refs),
        out_shape=(
            shape((per, 2 * tok, HD)),
            shape((2, group, HD)),
            shape((groups, STAT_ROWS, HD), F32),
        ),
        in_specs=[smem, whole, whole, whole],
        out_specs=(hbm, hbm, hbm),
        scratch_shapes=[
            pltpu.VMEM((per, 2 * tok, HD), BF16),
            pltpu.VMEM((2, group, HD), BF16),
            pltpu.VMEM((groups, STAT_ROWS, HD), F32),
            pltpu.SemaphoreType.DMA((3,)),
            pltpu.VMEM((total + PATCH_MOST, HD), F32),
            pltpu.VMEM((total + PATCH_MOST, HD), F32),
            pltpu.VMEM((total, HD), BF16),
            pltpu.VMEM((total, HD), BF16),
            pltpu.VMEM((group, HD), BF16),
            pltpu.VMEM((group, HD), BF16),
            pltpu.VMEM((most_chunks, group, CHUNK), F32),
            pltpu.VMEM((group, HD), F32),
            pltpu.VMEM((group, HD), F32),
            pltpu.VMEM((group, HD), F32),
        ],
        compiler_params=vmem(62),
        name="queries",
    )(meta, start, kv_all, q_mine)
    all_stats = lax.all_to_all(stats, "z", 0, 0, tiled=True)
    answers, all_stats = lax.optimization_barrier((answers, all_stats))
    returned = lax.all_to_all(answers, "y", 0, 0, tiled=True)
    att_here, dq_here = pl.pallas_call(
        lambda *refs: unpack_queries_kernel(heads, tok, *refs),
        out_shape=(shape((tok, cols)), shape((tok, cols))),
        in_specs=[whole],
        out_specs=(whole, whole),
        compiler_params=vmem(),
        name="unpack_queries",
    )(returned)
    q_all, returned = lax.optimization_barrier((q_all, returned))

    d_kv, key_grads = pl.pallas_call(
        lambda *refs: key_kernel(frames, tok, *refs),
        out_shape=(shape((group, 2 * HD)), shape((per, 2 * tok, HD))),
        in_specs=[smem, whole, hbm, hbm, hbm],
        out_specs=(hbm, hbm),
        scratch_shapes=[
            pltpu.VMEM((most_blocks * tok + KEY_CHUNK, HD), BF16),
            pltpu.VMEM((most_blocks * tok + KEY_CHUNK, HD), BF16),
            pltpu.VMEM((groups, STAT_ROWS, HD), F32),
            pltpu.VMEM((2, group, HD), BF16),
            pltpu.VMEM((group, HD), F32),
            pltpu.VMEM((group, HD), F32),
            pltpu.VMEM((group, 2 * HD), BF16),
            pltpu.VMEM((per, 2 * tok, HD), BF16),
            pltpu.SemaphoreType.DMA((most_blocks,)),
            pltpu.SemaphoreType.DMA((most_blocks,)),
            pltpu.SemaphoreType.DMA((2,)),
            pltpu.SemaphoreType.DMA((2,)),
        ],
        compiler_params=vmem(62),
        name="keys",
    )(meta, end, q_all, all_stats, own_kv)
    d_kv_all = lax.all_gather(d_kv, "z", axis=0, tiled=True)
    keys_back = lax.all_to_all(key_grads, "y", 0, 0, tiled=True)
    d_text_kv, terms = pl.pallas_call(
        lambda *refs: unpack_kernel(heads, tok, *refs),
        out_shape=(shape((2, tok, cols)), shape((sections, tok, width // sections))),
        in_specs=[smem] + [whole] * 4,
        out_specs=(whole,) * 2,
        compiler_params=vmem(),
        name="unpack",
    )(meta, image_offsets.reshape(1, frames), patch_counts.reshape(1, frames), keys_back, proj)

    summed = lax.all_to_all(terms, "phase", 0, 0, tiled=True)
    here = pl.pallas_call(
        sum_kernel,
        out_shape=shape((per, tok, HD)),
        in_specs=[whole],
        out_specs=whole,
        compiler_params=vmem(),
        name="sum",
    )(summed)
    of_group = lax.all_to_all(here, "y", 0, 0, tiled=True)
    routed = pl.pallas_call(
        lambda *refs: route_kernel(frames, *refs),
        out_shape=shape((groups, PATCH_MOST, HD)),
        in_specs=[smem, whole],
        out_specs=whole,
        scratch_shapes=[pltpu.VMEM((group + PATCH_MOST, HD), F32)],
        compiler_params=vmem(),
        name="route",
    )(meta, of_group)
    from_groups = lax.all_to_all(routed, "z", 0, 0, tiled=True)
    d_slice = pl.pallas_call(
        lambda *refs: pick_kernel(frames, group, *refs),
        out_shape=shape((sections, PATCH_MOST, HD)),
        in_specs=[smem, whole],
        out_specs=whole,
        compiler_params=vmem(),
        name="pick",
    )(meta, from_groups)
    d_normed = lax.all_to_all(d_slice, "phase", 0, 0, tiled=True)
    proj_rows = width // blocks
    proj_head = pl.pallas_call(
        proj_kernel,
        out_shape=shape((per, 2 * proj_rows, HD)),
        in_specs=[whole, whole],
        out_specs=whole,
        compiler_params=vmem(),
        name="proj_grad",
    )(norm_pos, d_kv_all)
    proj_back = lax.all_to_all(proj_head, "y", 0, 0, tiled=True)
    d_proj = pl.pallas_call(
        lambda *refs: proj_out_kernel(heads, *refs),
        out_shape=shape((proj_rows, 2, cols), F32),
        in_specs=[whole],
        out_specs=whole,
        compiler_params=vmem(),
        name="proj_out",
    )(proj_back)
    d_patches = pl.pallas_call(
        norm_grad_kernel,
        out_shape=shape(patches.shape),
        in_specs=[whole] * 3,
        out_specs=whole,
        compiler_params=vmem(),
        name="norm_grad",
    )(patches, gain, d_normed)
    return (
        att_here,
        dq_here,
        d_text_kv,
        d_proj,
        d_patches,
    )


def solution(mesh):
    sections, seq = mesh.devices.shape
    per = 4
    inner = Mesh(mesh.devices.reshape(sections, seq // per, per), ("phase", "z", "y"))
    seq = ("z", "y")
    return jax.shard_map(
        shards,
        mesh=inner,
        in_specs=(
            P(seq, None),
            P(),
            P(None, None, "phase"),
            P(seq, "phase"),
            P(None, seq, "phase"),
            P(None, "phase"),
            P(seq, "phase"),
            P(),
            P(),
            P(seq),
            P(),
        ),
        out_specs=(
            P(seq, "phase"),
            P(seq, "phase"),
            P(None, seq, "phase"),
            P(seq, None, "phase"),
            P(seq, None),
        ),
        check_vma=False,
    )
```

```python
import functools
import math

import jax
import jax.numpy as jnp
from jax import lax
from jax.experimental import pallas as pl
from jax.experimental.pallas import tpu as pltpu
from jax.sharding import Mesh
from jax.sharding import PartitionSpec as P

HD = 128
PAD = 256
PATCH_MOST = 64
EPISODES = 16
EPISODE_MOST = 2720
EPSILON = 1e-05
NEGATIVE = -1e30
CHUNK = 256
KEY_CHUNK = 512
STAT_ROWS = 16

F32 = jnp.float32
BF16 = jnp.bfloat16


def dot_nt(a, b):
    return lax.dot_general(a, b, (((1,), (1,)), ((), ())), preferred_element_type=F32)


def dot_tn(a, b):
    return lax.dot_general(a, b, (((0,), (0,)), ((), ())), preferred_element_type=F32)


def dot_nn(a, b):
    return jnp.dot(a, b, preferred_element_type=F32)


def normalize_rows(patches):
    row_values = patches.astype(F32)
    center = row_values - jnp.mean(row_values, axis=-1, keepdims=True)
    inverse = lax.rsqrt(jnp.mean(center * center, axis=-1, keepdims=True) + EPSILON)
    return (center * inverse, inverse)


def vmem(limit=48):
    return pltpu.CompilerParams(vmem_limit_bytes=limit * 1024 * 1024)


def pack_kernel(heads, tok, patch_ref, gain_ref, proj_ref, q_ref, kv_ref, bias_ref, do_ref, type_ref,
                kv_out, q_out, normed_ref):
    scaled, _ = normalize_rows(patch_ref[0:PATCH_MOST])
    normed = (scaled * gain_ref[...]).astype(BF16)
    for i in range(normed_ref.shape[0]):
        normed_ref[i] = normed[:, i * HD : (i + 1) * HD]
    image = dot_nn(normed, proj_ref[...]).astype(BF16)
    cols = heads * HD
    bias = jnp.where(type_ref[...] == 1, bias_ref[1:2].astype(F32), bias_ref[0:1].astype(F32))
    keys = (kv_ref[0].astype(F32) + bias).astype(BF16)
    for h in range(heads):
        span = slice(h * HD, (h + 1) * HD)
        kv_out[h, 0:tok] = keys[:, span]
        kv_out[h, tok : 2 * tok] = kv_ref[1, :, span]
        kv_out[h, 2 * tok : 2 * tok + PATCH_MOST] = image[:, span]
        kv_out[h, 2 * tok + PATCH_MOST :] = image[:, cols + h * HD : cols + (h + 1) * HD]
        q_out[h, 0:tok] = q_ref[:, span]
        q_out[h, tok:] = do_ref[:, span]
    for h in range(heads, kv_out.shape[0]):
        kv_out[h] = jnp.zeros_like(kv_out[h])
        q_out[h] = jnp.zeros_like(q_out[h])


def place_kernel(frames, meta_ref, rows_ref, out_ref, scratch):
    total = out_ref.shape[1]
    per = rows_ref.shape[0]
    scratch[...] = jnp.zeros_like(scratch)
    row = lax.broadcasted_iota(jnp.int32, (PATCH_MOST, HD), 0)

    def one(f, carry):
        where = pl.ds(meta_ref[f], PATCH_MOST)
        live = row < meta_ref[frames + f]
        rows = rows_ref[lax.rem(f, per), lax.div(f, per)].astype(F32)
        scratch[where] = jnp.where(live, rows, scratch[where])
        return carry

    lax.fori_loop(0, frames, one, 0)

    def low(c, carry):
        where = pl.ds(pl.multiple_of(c * CHUNK, CHUNK), CHUNK)
        out_ref[:, where] = jnp.transpose(scratch[where]).astype(BF16)
        return carry

    lax.fori_loop(0, total // CHUNK, low, 0)


def query_kernel(frames, tok, meta_ref, start_ref, g_ref, mine_ref, out_hbm, own_hbm, stat_hbm,
                 out_ref, own_ref, stat_ref, out_sem, kf, vf, kb, vb, qb, dob, s_ref, m_ref, l_ref, acc):
    group = own_ref.shape[1]
    total = kb.shape[0]
    scale = 1.0 / math.sqrt(HD)
    power = scale * math.log2(math.e)
    z = meta_ref[2 * frames]
    first_chunk = meta_ref[2 * frames + 2]
    last_chunk = meta_ref[2 * frames + 3]
    image_row = 2 * tok

    def text(b, carry):
        where = pl.ds(pl.multiple_of(b * tok, 32), tok)
        kf[where] = g_ref[b, 0:tok].astype(F32)
        vf[where] = g_ref[b, tok : 2 * tok].astype(F32)
        return carry

    lax.fori_loop(0, total // tok, text, 0)
    row = lax.broadcasted_iota(jnp.int32, (PATCH_MOST, HD), 0)

    def image(f, carry):
        where = pl.ds(meta_ref[f], PATCH_MOST)
        live = row < meta_ref[frames + f]
        kf[where] = jnp.where(live, g_ref[f, image_row : image_row + PATCH_MOST].astype(F32), kf[where])
        vf[where] = jnp.where(live, g_ref[f, image_row + PATCH_MOST :].astype(F32), vf[where])
        return carry

    lax.fori_loop(0, frames, image, 0)

    def low(c, carry):
        where = pl.ds(pl.multiple_of(c * CHUNK, CHUNK), CHUNK)
        kb[where] = kf[where].astype(BF16)
        vb[where] = vf[where].astype(BF16)
        return carry

    lax.fori_loop(0, total // CHUNK, low, 0)
    per = group // tok
    for i in range(per):
        qb[i * tok : (i + 1) * tok] = mine_ref[i, 0:tok]
        dob[i * tok : (i + 1) * tok] = mine_ref[i, tok:]
    own = pl.ds(pl.multiple_of(z * group, HD), group)
    own_ref[0] = kb[own]
    own_ref[1] = vb[own]
    own_copy = pltpu.make_async_copy(own_ref, own_hbm, out_sem.at[0])
    own_copy.start()

    m_ref[...] = jnp.full_like(m_ref, NEGATIVE)
    l_ref[...] = jnp.zeros_like(l_ref)
    acc[...] = jnp.zeros_like(acc)
    lane = lax.broadcasted_iota(jnp.int32, (group, CHUNK), 1)
    query_pos = z * group + lax.broadcasted_iota(jnp.int32, (group, 1), 0)
    start = start_ref[...]

    def chunk(c):
        return pl.ds(pl.multiple_of(c * CHUNK, CHUNK), CHUNK)

    def scores(c, carry):
        s = dot_nt(qb[...], kb[chunk(c)])
        pos = lane + c * CHUNK
        s = jnp.where((pos >= start) & (pos <= query_pos), s, NEGATIVE)
        s_ref[c - first_chunk] = s
        m_ref[...] = jnp.maximum(m_ref[...], jnp.maximum(s[:, :HD], s[:, HD:]))
        return carry

    lax.fori_loop(first_chunk, last_chunk, scores, 0)
    row_max = jnp.max(m_ref[...], axis=1, keepdims=True)
    m_ref[...] = jnp.broadcast_to(row_max, m_ref.shape)

    def weigh(c, carry):
        top = m_ref[...]
        w = jnp.exp2((s_ref[c - first_chunk] - jnp.concatenate([top, top], axis=1)) * power)
        s_ref[c - first_chunk] = w
        l_ref[...] += w[:, :HD] + w[:, HD:]
        acc[...] += dot_nn(w.astype(BF16), vb[chunk(c)])
        return carry

    lax.fori_loop(first_chunk, last_chunk, weigh, 0)
    inverse_sum = 1.0 / jnp.sum(l_ref[...], axis=1, keepdims=True)
    attended = (acc[...] * inverse_sum).astype(BF16)
    for i in range(per):
        out_ref[i, 0:tok] = attended[i * tok : (i + 1) * tok]
    delta = jnp.sum(dob[...].astype(F32) * attended.astype(F32), axis=1, keepdims=True)
    acc[...] = jnp.zeros_like(acc)
    m_ref[...] = jnp.broadcast_to(inverse_sum, m_ref.shape)
    l_ref[...] = jnp.broadcast_to(delta, l_ref.shape)

    def back(c, carry):
        d_prob = dot_nt(dob[...], vb[chunk(c)])
        inv, dlt = m_ref[...], l_ref[...]
        p = s_ref[c - first_chunk] * jnp.concatenate([inv, inv], axis=1)
        d_score = (p * (d_prob - jnp.concatenate([dlt, dlt], axis=1))).astype(BF16)
        acc[...] += dot_nn(d_score, kb[chunk(c)])
        return carry

    lax.fori_loop(first_chunk, last_chunk, back, 0)
    d_query = (acc[...] * scale).astype(BF16)
    for i in range(per):
        out_ref[i, tok:] = d_query[i * tok : (i + 1) * tok]
    which = lax.broadcasted_iota(jnp.int32, (group, HD), 1)
    table = jnp.where(which == 0, row_max, jnp.where(which == 1, inverse_sum, delta))
    tiles = [jnp.transpose(table[i * HD : (i + 1) * HD])[0:8] for i in range(group // HD)]
    stat = jnp.concatenate([t[k : k + 1] for k in range(3) for t in tiles], axis=0)
    stat = jnp.concatenate([stat, stat[0:1]], axis=0)
    for i in range(stat_ref.shape[0]):
        stat_ref[i] = stat
    stat_copy = pltpu.make_async_copy(stat_ref, stat_hbm, out_sem.at[1])
    out_copy = pltpu.make_async_copy(out_ref, out_hbm, out_sem.at[2])
    stat_copy.start()
    out_copy.start()
    own_copy.wait()
    stat_copy.wait()
    out_copy.wait()


def key_kernel(frames, tok, meta_ref, end_ref, g_hbm, stat_hbm, own_hbm, dkv_hbm, out_hbm,
               qb, dob, stat_ref, own_ref, dk, dv, rows_ref, out_ref, q_sem, do_sem, in_sem, out_sem):
    group = own_ref.shape[1]
    per = group // tok
    scale = 1.0 / math.sqrt(HD)
    power = scale * math.log2(math.e)
    z = meta_ref[2 * frames]
    count = meta_ref[2 * frames + 5]
    last_tile = stat_ref.shape[0] * (group // HD) - 1

    def fetch(i):
        where = pl.ds(pl.multiple_of(i * tok, 32), tok)
        b = z * per + i
        return (
            pltpu.make_async_copy(g_hbm.at[b, 0:tok], qb.at[where], q_sem.at[i]),
            pltpu.make_async_copy(g_hbm.at[b, tok : 2 * tok], dob.at[where], do_sem.at[i]),
        )

    own_copy = pltpu.make_async_copy(own_hbm, own_ref, in_sem.at[0])
    stat_copy = pltpu.make_async_copy(stat_hbm, stat_ref, in_sem.at[1])
    own_copy.start()
    stat_copy.start()

    def begin(i, carry):
        for copy in fetch(i):
            copy.start()
        return carry

    def finish(i, carry):
        for copy in fetch(i):
            copy.wait()
        return carry

    lax.fori_loop(0, count, begin, 0)
    dk[...] = jnp.zeros_like(dk)
    dv[...] = jnp.zeros_like(dv)
    tail = pl.ds(pl.multiple_of(count * tok, 32), KEY_CHUNK)
    qb[tail] = jnp.zeros((KEY_CHUNK, HD), BF16)
    dob[tail] = jnp.zeros((KEY_CHUNK, HD), BF16)
    lane = lax.broadcasted_iota(jnp.int32, (group, KEY_CHUNK), 1)
    key_pos = lax.broadcasted_iota(jnp.int32, (group, 1), 0)
    end = end_ref[...] - z * group
    own_copy.wait()
    stat_copy.wait()

    def statistics(c, kind):
        parts = []
        for half in range(KEY_CHUNK // HD):
            tile = jnp.minimum(z * (group // HD) + (KEY_CHUNK // HD) * c + half, last_tile)
            at = lax.div(tile, group // HD)
            row = kind * (group // HD) + lax.rem(tile, group // HD)
            parts.append(stat_ref[at, pl.ds(row, 1)])
        return jnp.concatenate(parts, axis=1)

    def step(masked, c, carry):
        where = pl.ds(pl.multiple_of(c * KEY_CHUNK, KEY_CHUNK), KEY_CHUNK)
        arrived = lax.div(c * KEY_CHUNK + tok - 1, tok)
        needed = jnp.minimum(lax.div((c + 1) * KEY_CHUNK + tok - 1, tok), count)
        lax.fori_loop(arrived, needed, finish, 0)
        q, do = qb[where], dob[where]
        s = dot_nt(own_ref[0], q)
        p = jnp.exp2((s - statistics(c, 0)) * power) * statistics(c, 1)
        if masked:
            pos = lane + c * KEY_CHUNK
            p = jnp.where((pos >= key_pos) & (pos < end), p, 0.0)
        dv[...] += dot_nn(p.astype(BF16), do)
        d_prob = dot_nt(own_ref[1], do)
        d_score = (p * (d_prob - statistics(c, 2))).astype(BF16)
        dk[...] += dot_nn(d_score, q)
        return carry

    chunks = meta_ref[2 * frames + 4]
    after = jnp.minimum((group + KEY_CHUNK - 1) // KEY_CHUNK, chunks)
    shared = jnp.maximum(meta_ref[2 * frames + 6], after)
    lax.fori_loop(0, after, functools.partial(step, True), 0)
    lax.fori_loop(after, shared, functools.partial(step, False), 0)
    lax.fori_loop(shared, chunks, functools.partial(step, True), 0)
    key_grad = (dk[...] * scale).astype(BF16)
    value_grad = dv[...].astype(BF16)
    rows_ref[:, 0:HD] = key_grad
    rows_ref[:, HD:] = value_grad
    rows_copy = pltpu.make_async_copy(rows_ref, dkv_hbm, out_sem.at[0])
    rows_copy.start()
    for i in range(per):
        rows = slice(i * tok, (i + 1) * tok)
        out_ref[i, 0:tok] = key_grad[rows]
        out_ref[i, tok:] = value_grad[rows]
    out_copy = pltpu.make_async_copy(out_ref, out_hbm, out_sem.at[1])
    out_copy.start()
    rows_copy.wait()
    out_copy.wait()


def proj_kernel(norm_ref, grad_ref, out_ref):
    total = dot_nn(norm_ref[...], grad_ref[...])
    low = total.astype(BF16)
    rows = out_ref.shape[1] // 2
    for i in range(out_ref.shape[0]):
        out_ref[i, 0:rows] = low[i * rows : (i + 1) * rows, 0:HD]
        out_ref[i, rows:] = low[i * rows : (i + 1) * rows, HD:]


def unpack_queries_kernel(heads, tok, r_ref, att_ref, dq_ref):
    for h in range(heads):
        span = slice(h * HD, (h + 1) * HD)
        att_ref[:, span] = r_ref[h, 0:tok]
        dq_ref[:, span] = r_ref[h, tok:]


def unpack_kernel(heads, tok, meta_ref, offset_ref, count_ref, r_ref, proj_ref, dtext_ref, dn_ref):
    frames = offset_ref.shape[1]
    pos = meta_ref[2 * frames + 1] * tok + lax.broadcasted_iota(jnp.int32, (tok, frames), 0)
    begin = offset_ref[...]
    inside = (pos >= begin) & (pos < begin + count_ref[...])
    is_image = jnp.max(inside.astype(F32), axis=1, keepdims=True) > 0.5
    parts = [None] * (2 * heads)
    for h in range(heads):
        span = slice(h * HD, (h + 1) * HD)
        for c in range(2):
            grad = r_ref[h, c * tok : (c + 1) * tok]
            zero = jnp.zeros_like(grad)
            dtext_ref[c, :, span] = jnp.where(is_image, zero, grad)
            parts[c * heads + h] = jnp.where(is_image, grad, zero)
    grads = jnp.concatenate(parts, axis=1)
    terms = dot_nt(grads, proj_ref[...]).astype(BF16)
    for i in range(dn_ref.shape[0]):
        dn_ref[i] = terms[:, i * HD : (i + 1) * HD]


def sum_kernel(dn_ref, out_ref):
    total = dn_ref[0].astype(F32)
    for i in range(1, dn_ref.shape[0]):
        total = total + dn_ref[i].astype(F32)
    low = total.astype(BF16)
    for i in range(out_ref.shape[0]):
        out_ref[i] = low


def route_kernel(frames, meta_ref, rows_ref, out_ref, scratch):
    per, tok = rows_ref.shape[0], rows_ref.shape[1]
    group = per * tok
    z = meta_ref[2 * frames]
    y = meta_ref[2 * frames + 1] - z * per
    for i in range(per):
        scratch[i * tok : (i + 1) * tok] = rows_ref[i].astype(F32)
    scratch[group:] = jnp.zeros((PATCH_MOST, HD), F32)
    row = lax.broadcasted_iota(jnp.int32, (PATCH_MOST, HD), 0)
    for i in range(out_ref.shape[0]):
        f = i * per + y
        offset = meta_ref[f] - z * group
        here = (offset >= 0) & (offset < group)
        live = jnp.where(here, meta_ref[frames + f], 0)
        rows = scratch[pl.ds(jnp.where(here, offset, 0), PATCH_MOST)]
        out_ref[i] = jnp.where(row < live, rows, 0.0).astype(BF16)


def pick_kernel(frames, group, meta_ref, rows_ref, out_ref):
    rows = rows_ref[lax.div(meta_ref[meta_ref[2 * frames + 1]], group)]
    for i in range(out_ref.shape[0]):
        out_ref[i] = rows


def proj_out_kernel(heads, r_ref, out_ref):
    rows = out_ref.shape[0]
    for h in range(heads):
        for c in range(2):
            part = r_ref[h, c * rows : (c + 1) * rows].astype(F32)
            out_ref[:, c, h * HD : (h + 1) * HD] = part


def norm_grad_kernel(patch_ref, gain_ref, dn_ref, out_ref):
    scaled, inverse = normalize_rows(patch_ref[0:PATCH_MOST])
    d_normed = jnp.concatenate([dn_ref[i] for i in range(dn_ref.shape[0])], axis=1).astype(F32)
    scaled_grad = d_normed * gain_ref[...]
    d_rows = (
        scaled_grad
        - jnp.mean(scaled_grad, axis=-1, keepdims=True)
        - scaled * jnp.mean(scaled_grad * scaled, axis=-1, keepdims=True)
    ) * inverse
    out_ref[0:PATCH_MOST] = d_rows.astype(BF16)
    out_ref[PATCH_MOST:] = jnp.zeros((out_ref.shape[0] - PATCH_MOST, out_ref.shape[1]), BF16)


def shards(patches, ln_gain, kv_proj, query, text_kv, type_bias, d_out, patch_counts, image_offsets,
           token_types, segment_ids):
    tok, cols = query.shape
    heads = cols // HD
    width = patches.shape[1]
    groups, per, sections = lax.axis_size("z"), lax.axis_size("y"), lax.axis_size("phase")
    frames = patch_counts.shape[0]
    blocks = groups * per
    group = per * tok
    total = blocks * tok
    z, y, section = lax.axis_index("z"), lax.axis_index("y"), lax.axis_index("phase")
    block = z * per + y
    smem = pl.BlockSpec(memory_space=pltpu.SMEM)
    whole = pl.BlockSpec(memory_space=pltpu.VMEM)
    hbm = pl.BlockSpec(memory_space=pltpu.HBM)

    def shape(dims, kind=BF16):
        return jax.ShapeDtypeStruct(dims, kind)

    ids = jnp.arange(EPISODES, dtype=jnp.int32)
    seg_first = jnp.sum((segment_ids[None, :] < ids[:, None]).astype(jnp.int32), axis=1)
    seg_end = jnp.sum((segment_ids[None, :] <= ids[:, None]).astype(jnp.int32), axis=1)
    own_seg = lax.dynamic_slice_in_dim(segment_ids, z * group, group)
    same = own_seg[:, None] == ids[None, :]
    start = jnp.sum(jnp.where(same, seg_first[None, :], 0), axis=1, keepdims=True)
    end = jnp.sum(jnp.where(same, seg_end[None, :], 0), axis=1, keepdims=True)
    scalars = jnp.stack([
        z,
        block,
        start[0, 0] // CHUNK,
        ((z + 1) * group + CHUNK - 1) // CHUNK,
        (end[group - 1, 0] - z * group + KEY_CHUNK - 1) // KEY_CHUNK,
        (end[group - 1, 0] - z * group + tok - 1) // tok,
        (end[0, 0] - z * group) // KEY_CHUNK,
    ]).astype(jnp.int32)
    meta = jnp.concatenate([image_offsets, patch_counts, scalars])
    gain = ln_gain.reshape(1, width)
    proj = kv_proj.reshape(width, 2 * cols)
    packed, questions, normed = pl.pallas_call(
        lambda *refs: pack_kernel(heads, tok, *refs),
        out_shape=(
            shape((per, 2 * tok + 2 * PATCH_MOST, HD)),
            shape((per, 2 * tok, HD)),
            shape((groups, PATCH_MOST, HD)),
        ),
        in_specs=[whole] * 8,
        out_specs=(whole, whole, whole),
        compiler_params=vmem(),
        name="pack",
    )(patches, gain, proj, query, text_kv, type_bias, d_out, token_types.reshape(tok, 1))
    kv_mine = lax.all_to_all(packed, "y", 0, 0, tiled=True)
    kv_all = lax.all_gather(kv_mine, "z", axis=0, tiled=True)
    questions, _ = lax.optimization_barrier((questions, kv_mine))
    q_mine = lax.all_to_all(questions, "y", 0, 0, tiled=True)
    q_all = lax.all_gather(q_mine, "z", axis=0, tiled=True)

    normed, _ = lax.optimization_barrier((normed, q_mine))
    some_frames = lax.all_to_all(normed, "z", 0, 0, tiled=True)
    all_frames = lax.all_gather(some_frames, "y", axis=0, tiled=False)
    norm_pos = pl.pallas_call(
        lambda *refs: place_kernel(frames, *refs),
        out_shape=shape((HD, total)),
        in_specs=[smem, whole],
        out_specs=whole,
        scratch_shapes=[pltpu.VMEM((total + PATCH_MOST, HD), F32)],
        compiler_params=vmem(),
        name="place",
    )(meta, all_frames)
    kv_all, norm_pos = lax.optimization_barrier((kv_all, norm_pos))

    most_blocks = (group - 1 + EPISODE_MOST + tok - 1) // tok
    most_chunks = (EPISODE_MOST + group + CHUNK - 2) // CHUNK + 1
    answers, own_kv, stats = pl.pallas_call(
        lambda *refs: query_kernel(frames, tok, *refs),
        out_shape=(
            shape((per, 2 * tok, HD)),
            shape((2, group, HD)),
            shape((groups, STAT_ROWS, HD), F32),
        ),
        in_specs=[smem, whole, whole, whole],
        out_specs=(hbm, hbm, hbm),
        scratch_shapes=[
            pltpu.VMEM((per, 2 * tok, HD), BF16),
            pltpu.VMEM((2, group, HD), BF16),
            pltpu.VMEM((groups, STAT_ROWS, HD), F32),
            pltpu.SemaphoreType.DMA((3,)),
            pltpu.VMEM((total + PATCH_MOST, HD), F32),
            pltpu.VMEM((total + PATCH_MOST, HD), F32),
            pltpu.VMEM((total, HD), BF16),
            pltpu.VMEM((total, HD), BF16),
            pltpu.VMEM((group, HD), BF16),
            pltpu.VMEM((group, HD), BF16),
            pltpu.VMEM((most_chunks, group, CHUNK), F32),
            pltpu.VMEM((group, HD), F32),
            pltpu.VMEM((group, HD), F32),
            pltpu.VMEM((group, HD), F32),
        ],
        compiler_params=vmem(62),
        name="queries",
    )(meta, start, kv_all, q_mine)
    all_stats = lax.all_to_all(stats, "z", 0, 0, tiled=True)
    answers, all_stats = lax.optimization_barrier((answers, all_stats))
    returned = lax.all_to_all(answers, "y", 0, 0, tiled=True)
    att_here, dq_here = pl.pallas_call(
        lambda *refs: unpack_queries_kernel(heads, tok, *refs),
        out_shape=(shape((tok, cols)), shape((tok, cols))),
        in_specs=[whole],
        out_specs=(whole, whole),
        compiler_params=vmem(),
        name="unpack_queries",
    )(returned)
    q_all, returned = lax.optimization_barrier((q_all, returned))

    d_kv, key_grads = pl.pallas_call(
        lambda *refs: key_kernel(frames, tok, *refs),
        out_shape=(shape((group, 2 * HD)), shape((per, 2 * tok, HD))),
        in_specs=[smem, whole, hbm, hbm, hbm],
        out_specs=(hbm, hbm),
        scratch_shapes=[
            pltpu.VMEM((most_blocks * tok + KEY_CHUNK, HD), BF16),
            pltpu.VMEM((most_blocks * tok + KEY_CHUNK, HD), BF16),
            pltpu.VMEM((groups, STAT_ROWS, HD), F32),
            pltpu.VMEM((2, group, HD), BF16),
            pltpu.VMEM((group, HD), F32),
            pltpu.VMEM((group, HD), F32),
            pltpu.VMEM((group, 2 * HD), BF16),
            pltpu.VMEM((per, 2 * tok, HD), BF16),
            pltpu.SemaphoreType.DMA((most_blocks,)),
            pltpu.SemaphoreType.DMA((most_blocks,)),
            pltpu.SemaphoreType.DMA((2,)),
            pltpu.SemaphoreType.DMA((2,)),
        ],
        compiler_params=vmem(62),
        name="keys",
    )(meta, end, q_all, all_stats, own_kv)
    d_kv_all = lax.all_gather(d_kv, "z", axis=0, tiled=True)
    keys_back = lax.all_to_all(key_grads, "y", 0, 0, tiled=True)
    d_text_kv, terms = pl.pallas_call(
        lambda *refs: unpack_kernel(heads, tok, *refs),
        out_shape=(shape((2, tok, cols)), shape((sections, tok, width // sections))),
        in_specs=[smem] + [whole] * 4,
        out_specs=(whole,) * 2,
        compiler_params=vmem(),
        name="unpack",
    )(meta, image_offsets.reshape(1, frames), patch_counts.reshape(1, frames), keys_back, proj)

    summed = lax.all_to_all(terms, "phase", 0, 0, tiled=True)
    here = pl.pallas_call(
        sum_kernel,
        out_shape=shape((per, tok, HD)),
        in_specs=[whole],
        out_specs=whole,
        compiler_params=vmem(),
        name="sum",
    )(summed)
    of_group = lax.all_to_all(here, "y", 0, 0, tiled=True)
    routed = pl.pallas_call(
        lambda *refs: route_kernel(frames, *refs),
        out_shape=shape((groups, PATCH_MOST, HD)),
        in_specs=[smem, whole],
        out_specs=whole,
        scratch_shapes=[pltpu.VMEM((group + PATCH_MOST, HD), F32)],
        compiler_params=vmem(),
        name="route",
    )(meta, of_group)
    from_groups = lax.all_to_all(routed, "z", 0, 0, tiled=True)
    d_slice = pl.pallas_call(
        lambda *refs: pick_kernel(frames, group, *refs),
        out_shape=shape((sections, PATCH_MOST, HD)),
        in_specs=[smem, whole],
        out_specs=whole,
        compiler_params=vmem(),
        name="pick",
    )(meta, from_groups)
    d_normed = lax.all_to_all(d_slice, "phase", 0, 0, tiled=True)
    proj_rows = width // blocks
    proj_head = pl.pallas_call(
        proj_kernel,
        out_shape=shape((per, 2 * proj_rows, HD)),
        in_specs=[whole, whole],
        out_specs=whole,
        compiler_params=vmem(),
        name="proj_grad",
    )(norm_pos, d_kv_all)
    proj_back = lax.all_to_all(proj_head, "y", 0, 0, tiled=True)
    d_proj = pl.pallas_call(
        lambda *refs: proj_out_kernel(heads, *refs),
        out_shape=shape((proj_rows, 2, cols), F32),
        in_specs=[whole],
        out_specs=whole,
        compiler_params=vmem(),
        name="proj_out",
    )(proj_back)
    d_patches = pl.pallas_call(
        norm_grad_kernel,
        out_shape=shape(patches.shape),
        in_specs=[whole] * 3,
        out_specs=whole,
        compiler_params=vmem(),
        name="norm_grad",
    )(patches, gain, d_normed)
    return (
        att_here,
        dq_here,
        d_text_kv,
        d_proj,
        d_patches,
    )


def solution(mesh):
    sections, seq = mesh.devices.shape
    per = 4
    inner = Mesh(mesh.devices.reshape(sections, seq // per, per), ("phase", "z", "y"))
    seq = ("z", "y")
    return jax.shard_map(
        shards,
        mesh=inner,
        in_specs=(
            P(seq, None),
            P(),
            P(None, None, "phase"),
            P(seq, "phase"),
            P(None, seq, "phase"),
            P(None, "phase"),
            P(seq, "phase"),
            P(),
            P(),
            P(seq),
            P(),
        ),
        out_specs=(
            P(seq, "phase"),
            P(seq, "phase"),
            P(None, seq, "phase"),
            P(seq, None, "phase"),
            P(seq, None),
        ),
        check_vma=False,
    )
```
